32 devices in a mesh: leaf: 8 (over z, x), rhs: 4 (over y, core).
Axes of the slice: x: 2, y: 2, z: 4, core: 2. Of those that a mesh axis runs over, the one named last changes fastest.
Arguments:
- points: bfloat16 [16384, 784], P('leaf'), may hold values from -8 to 8
- vectors: bfloat16 [16384, 128], P('leaf', 'rhs'), may hold values from -6 to 6
- bases: float32 [64, 256, 64], P('leaf'), may hold values from -0.375 to 0.375
- leaf_coupling: float32 [64, 8, 64, 64], P('leaf'), may hold values from -0.75 to 0.75
- transfer: float32 [64, 64, 64], P('leaf'), may hold values from -0.75 to 0.75
- up_coupling: float32 [32, 8, 64, 64], P('leaf'), may hold values from -0.75 to 0.75
- far_leaf: int32 [64, 8], P('leaf'), may hold values from 0 to 63, as said below
- far_up: int32 [32, 8], P('leaf'), may hold values from 0 to 31, as said below
- near_lists: int32 [64, 8], P('leaf'), may hold values from -1 to 63, as said below
Outputs:
- product: float32 [16384, 128], P('leaf', 'rhs')
The draws below stay inside these ranges and needn't reach their ends.
Inputs may be any that keep to these rules, and one draw needn't show every extreme that they name: `near_lists`: row i begins with i itself; the other entries are distinct leaves j with 0 < |i - j| <= 8, or -1 for an unused slot. `far_leaf`: each row holds 8 distinct leaves, each more than 8 away from the row's own leaf in index. `far_up`: each row holds 8 distinct parents, each at least 2 away from the row's own parent in index.
All inputs are finite; a program needn't handle non-finite values.
Results may differ from the reference program's by a relative error of at most 0.0025.
Values may be sent and summed in bfloat16 or wider, within the bound.
No kernel may reach another device: no remote copies, remote signals or barrier semaphores. Data moves between devices by JAX's collectives and lax.ppermute only.
A program may use at most 128 MiB of HBM per device.

```python
import math
import jax
import jax.numpy as jnp
from jax import lax

D = 784
LEAF_PTS = 256
RANK = 64
NRHS = 128
NEAR = 8
FAR = 8
FAR_UP = 8
LEAF_DEV = 8
LEAVES = 64
PARENTS = 32
POINTS = 16384


def draw_points(key, part):
    latent_dims = 8
    carry_rate = 0.84
    jitter_scale = 0.5
    subkeys = jax.random.split(jax.random.fold_in(key, 53), 4)
    shocks = jax.random.normal(subkeys[0], (LEAVES, latent_dims), jnp.float32)

    def advance(current, innovation):
        stepped = carry_rate * current + math.sqrt(1.0 - carry_rate * carry_rate) * innovation
        return (stepped, stepped)
    opening = shocks[0]
    unused, following = lax.scan(advance, opening, shocks[1:])
    centres = jnp.concatenate([opening[None, :], following], axis=0)
    offsets = jax.random.normal(subkeys[1], (LEAVES, LEAF_PTS, latent_dims), jnp.float32)
    jitter = jax.random.normal(subkeys[3], (POINTS, D), jnp.float32) * jitter_scale
    embedding = jax.random.normal(subkeys[2], (latent_dims, D), jnp.float32) / math.sqrt(latent_dims)
    latent = (centres[:, None, :] + offsets).reshape(POINTS, latent_dims)
    placed = jnp.dot(latent, embedding, precision=lax.Precision.HIGHEST) + jitter
    return jnp.clip(placed, -8.0, 8.0).astype(jnp.bfloat16)


def draw_near_lists(key, part):
    offsets = jnp.concatenate([jnp.arange(LEAF_DEV, dtype=jnp.int32) - LEAF_DEV, jnp.arange(LEAF_DEV, dtype=jnp.int32) + 1])
    subkeys = jax.random.split(jax.random.fold_in(key, 11), LEAVES)

    def pick_row(subkey):
        return jax.random.permutation(subkey, offsets)
    chosen = jax.vmap(pick_row)(subkeys)
    taken_count = min(NEAR - 1, 2 * LEAF_DEV)
    leaf_ids = jnp.arange(LEAVES, dtype=jnp.int32)
    others = leaf_ids[:, None] + chosen[:, :taken_count]
    others = jnp.where((others >= 0) & (others < LEAVES), others, -1).astype(jnp.int32)
    padding = -jnp.ones((LEAVES, NEAR - 1 - taken_count), jnp.int32)
    return jnp.concatenate([leaf_ids[:, None], others, padding], axis=1)


def draw_far_leaf(key, part):
    window = LEAVES - 2 * LEAF_DEV - 1
    subkeys = jax.random.split(jax.random.fold_in(key, 23), LEAVES)

    def pick_row(subkey):
        return jax.random.permutation(subkey, window)[:FAR].astype(jnp.int32)
    chosen = jax.vmap(pick_row)(subkeys)
    leaf_ids = jnp.arange(LEAVES, dtype=jnp.int32)
    return ((leaf_ids[:, None] + LEAF_DEV + 1 + chosen) % LEAVES).astype(jnp.int32)


def draw_far_up(key, part):
    window = PARENTS - 3
    subkeys = jax.random.split(jax.random.fold_in(key, 37), PARENTS)

    def pick_row(subkey):
        return jax.random.permutation(subkey, window)[:FAR_UP].astype(jnp.int32)
    chosen = jax.vmap(pick_row)(subkeys)
    parent_ids = jnp.arange(PARENTS, dtype=jnp.int32)
    return ((parent_ids[:, None] + 2 + chosen) % PARENTS).astype(jnp.int32)


def level_of(rng, shape, cuts, smallest, high):
    level, own = 1.0, jax.random.fold_in(rng, 6)
    for dim, shards_of in cuts:
        steps = jnp.exp(jax.random.uniform(jax.random.fold_in(own, dim), (shards_of,), jnp.float32, smallest / len(cuts), high / len(cuts)))
        level = level * jnp.repeat(steps, shape[dim] // shards_of).reshape([-1 if axis == dim else 1 for axis in range(len(shape))])
    return level


def noise(own_key, shape, width, limit, cuts=(), kind=jnp.bfloat16):
    values = width * jax.random.normal(own_key, shape, jnp.float32)
    if cuts:
        values = values * level_of(own_key, shape, cuts, -0.22, 0.18)
    return jnp.clip(values, -limit, limit).astype(kind)


def setup_inputs(seed: int = 0) -> dict:
    splits = jax.random.split(jax.random.key(seed), 10)
    points = draw_points(jax.random.fold_in(splits[9], 71), 0)
    vectors = noise(splits[1], (POINTS, NRHS), 1.0, 6.0, ((0, 8), (1, 4)))
    bases = noise(splits[2], (LEAVES, LEAF_PTS, RANK), LEAF_PTS ** -0.5, 0.375, ((0, 8),), jnp.float32)
    leaf_coupling = noise(splits[3], (LEAVES, FAR, RANK, RANK), RANK ** -0.5, 0.75, ((0, 8),), jnp.float32)
    transfer = noise(splits[4], (LEAVES, RANK, RANK), RANK ** -0.5, 0.75, ((0, 8),), jnp.float32)
    up_coupling = noise(splits[5], (PARENTS, FAR_UP, RANK, RANK), RANK ** -0.5, 0.75, ((0, 8),), jnp.float32)
    far_leaf = draw_far_leaf(jax.random.fold_in(splits[9], 71), 0)
    far_up = draw_far_up(jax.random.fold_in(splits[9], 71), 0)
    near_lists = draw_near_lists(jax.random.fold_in(splits[9], 71), 0)
    return dict(points=points, vectors=vectors, bases=bases, leaf_coupling=leaf_coupling, transfer=transfer, up_coupling=up_coupling, far_leaf=far_leaf, far_up=far_up, near_lists=near_lists)


HIGHEST = lax.Precision.HIGHEST


def reference(points, vectors, bases, leaf_coupling, transfer, up_coupling, far_leaf, far_up, near_lists):
    vec_float = vectors.astype(jnp.float32).reshape(LEAVES, LEAF_PTS, NRHS)
    coeffs = jnp.einsum("lpr,lpc->lrc", bases, vec_float, precision=HIGHEST)
    lifted = jnp.einsum("lba,lbc->lac", transfer, coeffs, precision=HIGHEST)
    parents = lifted.reshape(PARENTS, 2, RANK, NRHS).sum(axis=1)
    leaf_field = jnp.einsum("lkab,lkbc->lac", leaf_coupling, jnp.take(coeffs, far_leaf, axis=0), precision=HIGHEST)
    upper_field = jnp.einsum("qkab,qkbc->qac", up_coupling, jnp.take(parents, far_up, axis=0), precision=HIGHEST)
    pushed = jnp.einsum("lab,lbc->lac", transfer, jnp.repeat(upper_field, 2, axis=0), precision=HIGHEST)
    far_part = jnp.einsum("lpr,lrc->lpc", bases, leaf_field + pushed, precision=HIGHEST)
    far_part = far_part.reshape(POINTS, NRHS)
    square_sums = jnp.sum(jnp.square(points.astype(jnp.float32)), axis=1)
    offsets = jnp.arange(LEAF_PTS, dtype=jnp.int32)

    def near_leaf(leaf_index):
        slot_ids = near_lists[leaf_index]
        usable = slot_ids >= 0
        safe_ids = jnp.where(usable, slot_ids, 0).astype(jnp.int32)
        row_ids = (safe_ids[:, None] * LEAF_PTS + offsets[None, :]).reshape(-1)
        near_points = jnp.take(points, row_ids, axis=0)
        own_points = lax.dynamic_slice_in_dim(points, leaf_index * LEAF_PTS, LEAF_PTS, 0)
        own_sums = lax.dynamic_slice_in_dim(square_sums, leaf_index * LEAF_PTS, LEAF_PTS, 0)
        cross_terms = lax.dot_general(own_points, near_points, (((1,), (1,)), ((), ())), preferred_element_type=jnp.float32)
        distance = own_sums[:, None] + jnp.take(square_sums, row_ids)[None, :] - 2.0 * cross_terms
        column_mask = jnp.repeat(usable.astype(jnp.float32), LEAF_PTS)
        kernel = (jnp.exp(-distance / D) * column_mask[None, :]).astype(jnp.bfloat16)
        near_vectors = jnp.take(vectors, row_ids, axis=0)
        return jnp.dot(kernel, near_vectors, preferred_element_type=jnp.float32)

    near_part = lax.map(near_leaf, jnp.arange(LEAVES, dtype=jnp.int32)).reshape(POINTS, NRHS)
    return near_part + far_part + 0.5 * vectors.astype(jnp.float32)
```

```python
import functools
import math

import jax
import jax.numpy as jnp
from jax import lax
from jax.experimental import pallas as pl
from jax.experimental.pallas import tpu as pltpu
from jax.sharding import PartitionSpec as P

RIDGE = 0.5
LOG2E = math.log2(math.e)
F32 = jnp.float32
BF16 = jnp.bfloat16
NN = (((1,), (0,)), ((), ()))
NT = (((1,), (1,)), ((), ()))
VMEM = pl.BlockSpec(memory_space=pltpu.VMEM)
SMEM = pl.BlockSpec(memory_space=pltpu.SMEM)
MIB = 1 << 20


def dot(a, b, dims):
    return lax.dot_general(a, b, dims, preferred_element_type=F32)


def halves(x):
    high = x.astype(BF16)
    return high, (x - high.astype(F32)).astype(BF16)


def split_dot(a, b, dims):
    a_high, a_low = halves(a)
    b_high, b_low = halves(b)
    return dot(a_high, b_high, dims) + (dot(a_high, b_low, dims) + dot(a_low, b_high, dims))


def half_split_dot(a, b, dims):
    b_high, b_low = halves(b)
    return dot(a, b_high, dims) + dot(a, b_low, dims)


def pack_kernel(vec_ref, bases_ref, transfer_ref, vt_ref, msg_ref):
    leaves, pts, _ = bases_ref.shape
    coeffs = []
    lifted = []
    for leaf in range(leaves):
        vt = vec_ref[leaf * pts : (leaf + 1) * pts, :].astype(F32).T.astype(BF16)
        vt_ref[leaf] = vt
        coeffs.append(half_split_dot(vt, bases_ref[leaf], NN))
        lifted.append(split_dot(coeffs[-1], transfer_ref[leaf], NN))
    parents = [lifted[2 * q] + lifted[2 * q + 1] for q in range(leaves // 2)]
    entries = coeffs + parents
    for e in range(len(entries) // 2):
        msg_ref[e] = jnp.concatenate(entries[2 * e : 2 * e + 2], axis=1).astype(BF16)


def scaled_sums(x, features):
    sums = jnp.sum(jnp.square(x.astype(F32)), axis=1, keepdims=True) * (LOG2E / features)
    return jnp.broadcast_to(sums, (x.shape[0], 128))


def row_of(sums):
    return sums.T[0:1, :]


def near_tile(x_a, x_b, sums_a, row_b):
    pts, features = x_a.shape
    cross = dot(x_a, x_b, NT) * (2.0 * LOG2E / features)
    wide = jnp.concatenate([sums_a] * (pts // 128), axis=1)
    return jnp.exp2(cross - (wide + row_b)).astype(BF16)


def listed(lists_ref, row, leaf):
    found = lists_ref[row, 0] == leaf
    for k in range(1, lists_ref.shape[1]):
        found = found | (lists_ref[row, k] == leaf)
    return found


def block_order(count):
    bits = count.bit_length() - 1
    return [int(format(m, "b").zfill(bits)[::-1], 2) if bits else 0 for m in range(count)]


def fill_vectors(piece_refs, v_ref):
    cols = piece_refs[0].shape[1]
    count = v_ref.shape[1] // cols
    where = {}
    for piece in piece_refs:
        for part in range(piece.shape[1] // cols):
            where[len(where)] = (piece, part)
    for spot, m in enumerate(block_order(count)):
        piece, part = where[m]
        v_ref[:, spot * cols : (spot + 1) * cols, :] = piece[:, part * cols : (part + 1) * cols, :]


def own_kernel(pieces, sc_ref, lists_ref, x_ref, *refs):
    piece_refs, (acc_ref, sums_ref, v_ref) = refs[:pieces], refs[pieces:]
    leaves = acc_ref.shape[0]
    pts = x_ref.shape[0] // leaves
    features = x_ref.shape[1]
    base = sc_ref[2]
    fill_vectors(piece_refs, v_ref)
    for leaf in range(leaves):
        sums_ref[leaf] = scaled_sums(x_ref[leaf * pts : (leaf + 1) * pts, :], features)
    acc_ref[...] = jnp.zeros_like(acc_ref)
    low, high = sc_ref[0], sc_ref[1]
    for step in range(leaves + 1):
        first = step <= low
        b = jnp.where(first, low, high)
        a = jnp.where(first, step, step - low - 1)
        x_a = x_ref[pl.ds(pl.multiple_of(a * pts, pts), pts), :]
        x_b = x_ref[pl.ds(pl.multiple_of(b * pts, pts), pts), :]
        tile = near_tile(x_a, x_b, sums_ref[a], row_of(sums_ref[b]))
        from_b = listed(lists_ref, a, base + b).astype(F32)
        from_a = (listed(lists_ref, b, base + a) & (a != b)).astype(F32)
        acc_ref[a] += from_b * dot(v_ref[b], tile, NT)
        acc_ref[b] += from_a * dot(v_ref[a], tile, NN)


def cross_kernel(
    pieces, start, sc_ref, lists_ref, next_lists_ref, x_ref, halo_ref, sums_ref, halo_v_ref, *refs
):
    part = 0 if start == 0 else 1
    piece_refs, refs = refs[:pieces], refs[pieces:]
    leaves = sums_ref.shape[0]
    half = leaves // 2
    groups = [g for g in (0, 1) if g * half >= start]
    ins, outs = refs[: 2 * len(groups)], refs[2 * len(groups) : 4 * len(groups)]
    ret_ref, v_ref = refs[-2:]
    pts = x_ref.shape[0] // leaves
    features = x_ref.shape[1]
    rows = v_ref.shape[1]
    base = sc_ref[2]
    b = sc_ref[part]
    fill_vectors(piece_refs, v_ref)
    for source, target in zip(ins, outs):
        target[...] = source[...]
    ret_ref[...] = jnp.zeros_like(ret_ref)
    row_b = row_of(scaled_sums(halo_ref[...], features))
    for a in range(start, leaves):
        to_a = listed(lists_ref, a, base + leaves + b)
        to_b = listed(next_lists_ref, b, base + a)

        @pl.when((a >= b) & (to_a | to_b))
        def _():
            x_a = x_ref[a * pts : (a + 1) * pts, :]
            tile = near_tile(x_a, halo_ref[...], sums_ref[a], row_b)
            update = to_a.astype(F32) * dot(halo_v_ref[...], tile, NT)
            group = groups.index(a // half)
            outs[2 * group][a % half] += update[: rows // 2]
            outs[2 * group + 1][a % half] += update[rows // 2 :]
            ret_ref[...] += to_b.astype(F32) * dot(v_ref[a], tile, NN)


def far_kernel(
    sc_ref, far_leaf_ref, far_up_ref, all_ref, coupling_ref, up_ref, transfer_ref, bases_ref,
    vt_ref, out_ref
):
    leaves, _, rank = bases_ref.shape
    device = sc_ref[3]

    def entry(index, per_device, first):
        owner = lax.div(index, per_device)
        local = lax.rem(index, per_device)
        pair = all_ref[owner ^ device, first + lax.div(local, 2)].astype(F32)
        swapped = pltpu.roll(pair, rank, 1)
        return jnp.where(lax.rem(local, 2) == 1, swapped, pair)[:, :rank].astype(BF16)

    def field(list_ref, row, matrix_ref, per_device, first):
        total = None
        for k in range(list_ref.shape[1]):
            c = entry(list_ref[row, k], per_device, first)
            both = jnp.concatenate(halves(matrix_ref[row, k]), axis=0)
            term = dot(c, both, NT)
            total = term if total is None else total + term
        return total[:, :rank] + total[:, rank:]

    for parent in range(leaves // 2):
        upper = field(far_up_ref, parent, up_ref, leaves // 2, leaves // 2)
        for leaf in (2 * parent, 2 * parent + 1):
            total = field(far_leaf_ref, leaf, coupling_ref, leaves, 0)
            total = total + split_dot(upper, transfer_ref[leaf], NT)
            far = split_dot(total, bases_ref[leaf], NT)
            out_ref[leaf] = far + RIDGE * vt_ref[leaf].astype(F32)


def finish_kernel(low_ref, low_in_ref, high_ref, high_in_ref, far_ref, out_ref):
    half = low_ref.shape[0]
    pts = far_ref.shape[2]
    for leaf in range(2 * half):
        kept, came = (low_ref, low_in_ref) if leaf < half else (high_ref, high_in_ref)
        total = far_ref[leaf] + (kept[leaf % half] + came[leaf % half].astype(F32))
        out_ref[leaf * pts : (leaf + 1) * pts, :] = total.T


def call(body, out_shape, in_specs, args, flops=0, bytes_accessed=0, scratch=(), name=None):
    return pl.pallas_call(
        body,
        out_shape=out_shape,
        in_specs=in_specs,
        out_specs=jax.tree.map(lambda _: VMEM, out_shape),
        scratch_shapes=list(scratch),
        compiler_params=pltpu.CompilerParams(vmem_limit_bytes=40 * MIB),
        cost_estimate=pl.CostEstimate(
            flops=flops, bytes_accessed=bytes_accessed, transcendentals=0
        ),
        name=name,
    )(*args)


def xor_pairs(count, bit):
    return [(i, i ^ bit) for i in range(count)]


def local(
    points, vectors, bases, leaf_coupling, transfer, up_coupling, far_leaf, far_up, near_lists
):
    leaves, pts, rank = bases.shape
    cols = vectors.shape[1]
    half = leaves // 2
    shape = jax.ShapeDtypeStruct
    leaf_devices = lax.axis_size("leaf")
    rhs_devices = lax.axis_size("rhs")
    assert leaves == 2 * rhs_devices
    rows = cols * rhs_devices
    device = lax.axis_index("leaf")
    column = lax.axis_index("rhs")
    low, high = column, leaves - 1 - column
    down = [(i + 1, i) for i in range(leaf_devices - 1)]
    up = [(i, i + 1) for i in range(leaf_devices - 1)]
    scalars = jnp.stack([low, high, device * leaves, device]).astype(jnp.int32)

    def picked(array, leaf):
        return lax.dynamic_slice_in_dim(array, leaf * pts, pts, 0)

    halo_low = lax.ppermute(picked(points, low), "leaf", down)
    halo_high = lax.ppermute(picked(points, high), "leaf", down)
    next_lists = lax.ppermute(near_lists, "leaf", down)

    vt, message = call(
        pack_kernel,
        (
            shape((leaves, cols, pts), BF16),
            shape((half + half // 2, cols, 2 * rank), BF16),
        ),
        [VMEM] * 3,
        (vectors, bases, transfer),
        flops=10**8,
        bytes_accessed=3 * MIB,
        name="pack",
    )

    pieces = [vt]
    bit = 1
    while bit < rhs_devices:
        mine = pieces[0] if bit == 1 else jnp.concatenate(pieces, axis=1)
        pieces.append(lax.ppermute(mine, "rhs", xor_pairs(rhs_devices, bit)))
        bit *= 2

    everything = message[None]
    bit = 1
    while bit < leaf_devices:
        arrived = lax.ppermute(everything, "leaf", xor_pairs(leaf_devices, bit))
        everything = jnp.concatenate([everything, arrived], axis=0)
        bit *= 2

    def stacked(leaf):
        blocks = []
        for piece in pieces:
            chosen = lax.dynamic_index_in_dim(piece, leaf, 0, keepdims=False)
            blocks += [chosen[i : i + cols] for i in range(0, chosen.shape[0], cols)]
        return jnp.concatenate([blocks[m] for m in block_order(rhs_devices)], axis=0)

    halo_vectors = lax.ppermute(jnp.stack([stacked(low), stacked(high)]), "leaf", down)

    v_scratch = pltpu.VMEM((leaves, rows, pts), BF16)
    acc, sums = call(
        functools.partial(own_kernel, len(pieces)),
        (shape((leaves, rows, pts), F32), shape((leaves, pts, 128), F32)),
        [SMEM, SMEM] + [VMEM] * (1 + len(pieces)),
        (scalars, near_lists, points, *pieces),
        flops=3 * 10**9,
        bytes_accessed=6 * MIB,
        scratch=[v_scratch],
        name="own_tiles",
    )

    part = shape((half, rows // 2, pts), F32)
    back = shape((rows, pts), F32)

    def cross(start, halo, halo_v, totals):
        return call(
            functools.partial(cross_kernel, len(pieces), start),
            (part,) * len(totals) + (back,),
            [SMEM] * 3 + [VMEM] * (4 + len(pieces) + len(totals)),
            (scalars, near_lists, next_lists, points, halo, sums, halo_v, *pieces, *totals),
            flops=2 * 10**9,
            bytes_accessed=8 * MIB,
            scratch=[v_scratch],
            name="cross_tiles",
        )

    def reduced(keep, send, came, leaf):
        here = lax.iota(jnp.int32, half)[:, None, None] == leaf
        send = send + jnp.where(here, came[None, rows // 2 :], 0.0)
        keep = keep + jnp.where(here, came[None, : rows // 2], 0.0)
        bit = 1
        while True:
            arrived = lax.ppermute(send, "rhs", xor_pairs(rhs_devices, bit))
            bit *= 2
            if bit == rhs_devices:
                return keep, arrived
            total = keep + arrived.astype(F32)
            middle = total.shape[1] // 2
            keep, send = total[:, :middle], total[:, middle:].astype(BF16)

    totals = [
        acc[:half, : rows // 2], acc[:half, rows // 2 :],
        acc[half:, : rows // 2], acc[half:, rows // 2 :],
    ]
    keep_low, send_low, keep_high, send_high, back_low = cross(
        0, halo_low, halo_vectors[0], totals
    )
    came_low = lax.ppermute(back_low.astype(BF16), "leaf", up).astype(F32)
    low_parts = reduced(keep_low, send_low, came_low, low)
    keep_high, send_high, back_high = cross(
        half, halo_high, halo_vectors[1], [keep_high, send_high]
    )
    came_high = lax.ppermute(back_high.astype(BF16), "leaf", up).astype(F32)
    high_parts = reduced(keep_high, send_high, came_high, high - half)

    far = call(
        far_kernel,
        shape((leaves, cols, pts), F32),
        [SMEM] * 3 + [VMEM] * 6,
        (
            scalars, far_leaf, far_up, everything, leaf_coupling, up_coupling, transfer, bases,
            vt,
        ),
        flops=10**9,
        bytes_accessed=6 * MIB,
        name="far_field",
    )
    return call(
        finish_kernel,
        shape((leaves * pts, cols), F32),
        [VMEM] * 5,
        (*low_parts, *high_parts, far),
        bytes_accessed=2 * MIB,
        name="finish",
    )


def solution(mesh):
    return jax.shard_map(
        local,
        mesh=mesh,
        in_specs=(
            P("leaf", None),
            P("leaf", "rhs"),
            P("leaf", None, None),
            P("leaf", None, None, None),
            P("leaf", None, None),
            P("leaf", None, None, None),
            P("leaf", None),
            P("leaf", None),
            P("leaf", None),
        ),
        out_specs=P("leaf", "rhs"),
        check_vma=False,
    )
```

```python
import functools
import math

import jax
import jax.numpy as jnp
from jax import lax
from jax.experimental import pallas as pl
from jax.experimental.pallas import tpu as pltpu
from jax.sharding import PartitionSpec as P

RIDGE = 0.5
LOG2E = math.log2(math.e)
FLAG_ROWS = 16
F32 = jnp.float32
BF16 = jnp.bfloat16
NN = (((1,), (0,)), ((), ()))
NT = (((1,), (1,)), ((), ()))
VMEM = pl.BlockSpec(memory_space=pltpu.VMEM)
SMEM = pl.BlockSpec(memory_space=pltpu.SMEM)
MIB = 1 << 20


def dot(a, b, dims):
    return lax.dot_general(a, b, dims, preferred_element_type=F32)


def halves(x):
    high = x.astype(BF16)
    return high, (x - high.astype(F32)).astype(BF16)


def split_dot(a, b, dims):
    a_high, a_low = halves(a)
    b_high, b_low = halves(b)
    return dot(a_high, b_high, dims) + (dot(a_high, b_low, dims) + dot(a_low, b_high, dims))


def half_split_dot(a, b, dims):
    b_high, b_low = halves(b)
    return dot(a, b_high, dims) + dot(a, b_low, dims)


def span(index, size):
    return pl.ds(pl.multiple_of(index * size, size), size)


def listed(lists_ref, row, leaf):
    found = lists_ref[row, 0] == leaf
    for k in range(1, lists_ref.shape[1]):
        found = found | (lists_ref[row, k] == leaf)
    return found


def pack_kernel(v_ref, bases_ref, transfer_ref, msg_ref):
    leaves, _, pts = bases_ref.shape
    coeffs = []
    lifted = []
    for leaf in range(leaves):
        v = v_ref[:, leaf * pts : (leaf + 1) * pts]
        coeffs.append(half_split_dot(v, bases_ref[leaf], NT))
        lifted.append(split_dot(coeffs[-1], transfer_ref[leaf], NN))
    parents = [lifted[2 * q] + lifted[2 * q + 1] for q in range(leaves // 2)]
    entries = coeffs + parents
    for e in range(len(entries) // 2):
        msg_ref[e] = jnp.concatenate(entries[2 * e : 2 * e + 2], axis=1).astype(BF16)


def assemble_kernel(leaves, sc_ref, lists_ref, x_ref, *refs):
    piece_refs, (v_ref, down_ref, up_ref) = refs[:-3], refs[-3:]
    features, points = x_ref.shape
    pts = points // leaves
    rows = v_ref.shape[0]
    cols = piece_refs[0].shape[0]
    even = [piece_refs[0][...]] + [p[:cols] for p in piece_refs[2:]]
    odd = [piece_refs[1][...]] + [p[cols:] for p in piece_refs[2:]]
    for spot, block in enumerate(even + odd):
        v_ref[spot * cols : (spot + 1) * cols] = block
    low, upper, base = sc_ref[0], sc_ref[2], sc_ref[3]

    def flags(leaf, first):
        found = [
            jnp.full((1, pts), listed(lists_ref, leaf, first + a).astype(F32))
            for a in range(leaves)
        ]
        found.append(jnp.zeros((FLAG_ROWS - leaves, pts), F32))
        return jnp.concatenate(found, axis=0).astype(BF16)

    down_ref[:rows] = v_ref[:, span(low, pts)]
    down_ref[rows:] = flags(low, base - leaves)
    up_ref[:features] = x_ref[:, span(upper, pts)]
    up_ref[features : features + rows] = v_ref[:, span(upper, pts)]
    up_ref[features + rows :] = flags(upper, base + leaves)


def row_sums(x, features):
    return jnp.sum(jnp.square(x.astype(F32)), axis=0, keepdims=True) * (LOG2E / features)


def tiles(x_b, x, col, row, features):
    cross = dot(x_b, x, NN) * (2.0 * LOG2E / features)
    return jnp.exp2(cross - (col + row)).astype(BF16)


def column_sums(x_b, features):
    return jnp.sum(jnp.square(x_b.astype(F32)), axis=1, keepdims=True) * (LOG2E / features)


def mask_row(flags, pts):
    return jnp.concatenate([jnp.full((1, pts), f.astype(F32)) for f in flags], axis=1)


def own_kernel(leaves, sc_ref, lists_ref, x_ref, v_ref, *refs):
    out_refs, sums_ref = refs[:4], refs[4]
    features, points = x_ref.shape
    pts = points // leaves
    rows = v_ref.shape[0]
    low, high, base = sc_ref[0], sc_ref[1], sc_ref[3]
    for leaf in range(leaves):
        here = slice(leaf * pts, (leaf + 1) * pts)
        sums_ref[:, here] = jnp.broadcast_to(
            row_sums(x_ref[:, here], features), (sums_ref.shape[0], pts)
        )
    half = leaves // 2
    updates = [None, None]
    x_bs = [x_ref[:, span(b, pts)].T for b in (high, low)]
    cols = [column_sums(x_b, features) for x_b in x_bs]
    for group in (1, 0):
        here = slice(group * half * pts, (group + 1) * half * pts)
        total = None
        for which, b in enumerate((high, low)[: 2 - group]):
            tile = tiles(x_bs[which], x_ref[:, here], cols[which], sums_ref[0:1, here], features)
            leaf_ids = [group * half + i for i in range(half)]
            to_a = [(a <= b) & listed(lists_ref, a, base + b) for a in leaf_ids]
            to_b = [(a < b) & listed(lists_ref, b, base + a) for a in leaf_ids]
            term = dot(v_ref[:, span(b, pts)], tile, NN) * mask_row(to_a, pts)
            total = term if total is None else total + term
            masked = v_ref[:, here] * mask_row(to_b, pts).astype(BF16)
            back = dot(masked, tile, NT)
            updates[which] = back if updates[which] is None else updates[which] + back
        out_refs[2 * group][...] = total[: rows // 2]
        out_refs[2 * group + 1][...] = total[rows // 2 :]
    for b, back, group in ((high, updates[0], 1), (low, updates[1], 0)):
        place = span(b - group * half, pts)
        out_refs[2 * group][:, place] += back[: rows // 2]
        out_refs[2 * group + 1][:, place] += back[rows // 2 :]


def low_kernel(
    leaves, sc_ref, lists_ref, x_ref, halo_ref, near_ref, sums_ref, v_ref, *refs
):
    ins, outs, back_ref = refs[:4], refs[4:8], refs[8]
    features, points = x_ref.shape
    pts = points // leaves
    rows = v_ref.shape[0]
    half = leaves // 2
    b, base = sc_ref[0], sc_ref[3]
    x_b = halo_ref[...].T
    col = column_sums(x_b, features)
    back = None
    for group in (0, 1):
        here = slice(group * half * pts, (group + 1) * half * pts)
        leaf_ids = [group * half + i for i in range(half)]
        tile = tiles(x_b, x_ref[:, here], col, sums_ref[0:1, here], features)
        to_a = [(a >= b) & listed(lists_ref, a, base + leaves + b) for a in leaf_ids]
        term = dot(near_ref[:rows], tile, NN) * mask_row(to_a, pts)
        outs[2 * group][...] = ins[2 * group][...] + term[: rows // 2]
        outs[2 * group + 1][...] = ins[2 * group + 1][...] + term[rows // 2 :]
        to_b = jnp.concatenate([near_ref[rows + a : rows + a + 1, :] for a in leaf_ids], axis=1)
        to_b = to_b * mask_row([a >= b for a in leaf_ids], pts).astype(BF16)
        term = dot(v_ref[:, here] * to_b, tile, NT)
        back = term if back is None else back + term
    back_ref[...] = back.astype(back_ref.dtype)


def high_kernel(leaves, sc_ref, lists_ref, x_ref, halo_ref, sums_ref, v_ref, *refs):
    ins, outs = refs[:2], refs[2:]
    features, points = x_ref.shape
    pts = points // leaves
    rows = v_ref.shape[0]
    half = leaves // 2
    b, base = sc_ref[2], sc_ref[3]
    x_b = halo_ref[:features].T
    col = column_sums(x_b, features)
    here = slice(half * pts, leaves * pts)
    leaf_ids = [half + i for i in range(half)]
    tile = tiles(x_b, x_ref[:, here], col, sums_ref[0:1, here], features)
    to_a = [(a <= b) & listed(lists_ref, a, base - leaves + b) for a in leaf_ids]
    term = dot(halo_ref[features : features + rows], tile, NN) * mask_row(to_a, pts)
    first = features + rows
    to_b = jnp.concatenate([halo_ref[first + a : first + a + 1, :] for a in leaf_ids], axis=1)
    to_b = to_b * mask_row([a <= b for a in leaf_ids], pts).astype(BF16)
    back = dot(v_ref[:, here] * to_b, tile, NT)
    for i in (0, 1):
        block = slice(i * rows // 2, (i + 1) * rows // 2)
        outs[i][:, : half * pts] = ins[i][...] + term[block]
        outs[i][:, half * pts :] = back[block]


def merge_kernel(sc_ref, keep_ref, send_ref, back_ref, keep_out_ref, send_out_ref):
    rows, pts = back_ref.shape
    keep_out_ref[...] = keep_ref[...]
    send_out_ref[...] = send_ref[...]
    place = span(sc_ref[0], pts)
    keep_out_ref[:, place] += back_ref[: rows // 2].astype(F32)
    send_out_ref[:, place] += back_ref[rows // 2 :].astype(F32)


def split_kernel(backs, keep_ref, came_ref, out_ref, *refs):
    cols, wide = out_ref.shape
    blocks = keep_ref.shape[0] // cols
    pts = keep_ref.shape[1] - wide
    for m in range(blocks):
        block = slice(m * cols, (m + 1) * cols)
        total = keep_ref[block, :wide] + came_ref[block, :wide]
        if m == 0:
            out_ref[...] = total
        else:
            refs[m - 1][...] = total.astype(BF16)
        if backs:
            refs[blocks - 1 + m][:, :pts] = keep_ref[block, wide:].astype(BF16)
            refs[blocks - 1 + m][:, pts:] = came_ref[block, wide:].astype(BF16)


def far_kernel(
    sc_ref, far_leaf_ref, far_up_ref, all_ref, coupling_ref, up_ref, transfer_ref, bases_ref,
    v_ref, out_ref
):
    leaves, rank, pts = bases_ref.shape
    device = sc_ref[4]

    def entry(index, per_device, first):
        owner = lax.div(index, per_device)
        place = lax.rem(index, per_device)
        pair = all_ref[owner ^ device, first + lax.div(place, 2)].astype(F32)
        swapped = pltpu.roll(pair, rank, 1)
        return jnp.where(lax.rem(place, 2) == 1, swapped, pair)[:, :rank].astype(BF16)

    def field(list_ref, row, matrix_ref, per_device, first):
        total = None
        for k in range(list_ref.shape[1]):
            c = entry(list_ref[row, k], per_device, first)
            both = jnp.concatenate(halves(matrix_ref[row, k]), axis=0)
            term = dot(c, both, NT)
            total = term if total is None else total + term
        return total[:, :rank] + total[:, rank:]

    for parent in range(leaves // 2):
        upper = field(far_up_ref, parent, up_ref, leaves // 2, leaves // 2)
        for leaf in (2 * parent, 2 * parent + 1):
            total = field(far_leaf_ref, leaf, coupling_ref, leaves, 0)
            total = total + split_dot(upper, transfer_ref[leaf], NT)
            here = slice(leaf * pts, (leaf + 1) * pts)
            far = split_dot(total, bases_ref[leaf], NN)
            out_ref[:, here] = far + RIDGE * v_ref[:, here].astype(F32)


def finish_kernel(blocks, sc_ref, far_ref, *refs):
    out_ref = refs[-1]
    low_refs, high_refs = refs[:blocks], refs[blocks : 2 * blocks]
    back_refs = refs[2 * blocks : 3 * blocks]
    wide = low_refs[0].shape[1]
    pts = back_refs[0].shape[1] // 2
    column = sc_ref[0]
    for group, part_refs in enumerate((low_refs, high_refs)):
        here = slice(group * wide, (group + 1) * wide)
        total = part_refs[0][...]
        for ref in part_refs[1:]:
            total = total + ref[...].astype(F32)
        out_ref[:, here] = far_ref[:, here] + total
    for m in range(blocks):
        for core in (0, 1):
            place = span((column ^ (2 * m + core)) + wide // pts, pts)
            out_ref[:, place] += back_refs[m][:, core * pts : (core + 1) * pts].astype(F32)


def call(body, out_shape, in_specs, args, name, flops=0, bytes_accessed=0):
    return pl.pallas_call(
        body,
        out_shape=out_shape,
        in_specs=in_specs,
        out_specs=jax.tree.map(lambda _: VMEM, out_shape),
        compiler_params=pltpu.CompilerParams(vmem_limit_bytes=32 * MIB),
        cost_estimate=pl.CostEstimate(
            flops=flops, bytes_accessed=bytes_accessed, transcendentals=0
        ),
        name=name,
    )(*args)


def local(
    points, vectors, bases, leaf_coupling, transfer, up_coupling, far_leaf, far_up, near_lists
):
    leaves, pts, rank = bases.shape
    features = points.shape[1]
    cols = vectors.shape[1]
    half = leaves // 2
    shape = jax.ShapeDtypeStruct
    leaf_devices = lax.axis_size("leaf")
    rhs_devices = lax.axis_size("rhs")
    assert leaves == 2 * rhs_devices and leaves <= FLAG_ROWS
    rows = cols * rhs_devices
    wide = half * pts
    device = lax.axis_index("leaf")
    column = lax.axis_index("rhs")
    low, high, upper = column, leaves - 1 - column, half + column
    scalars = jnp.stack([low, high, upper, device * leaves, device]).astype(jnp.int32)

    def over_rhs(array, mask):
        return lax.ppermute(array, "rhs", [(i, i ^ mask) for i in range(rhs_devices)])

    def over_leaf(array, step, mask=0):
        pairs = [
            (i * rhs_devices + j, (i + step) * rhs_devices + (j ^ mask))
            for i in range(leaf_devices)
            if 0 <= i + step < leaf_devices
            for j in range(rhs_devices)
        ]
        return lax.ppermute(array, ("leaf", "rhs"), pairs)

    x = points.T
    v = vectors.T
    bases_t = jnp.swapaxes(bases, 1, 2)

    halo_low = over_leaf(lax.dynamic_slice_in_dim(x, low * pts, pts, 1), -1)
    v_other = over_rhs(v, 1)
    both = jnp.concatenate([v, v_other], axis=0)
    pieces = [v, v_other] + [over_rhs(both, m) for m in range(2, rhs_devices, 2)]

    message = call(
        pack_kernel,
        shape((half + half // 2, cols, 2 * rank), BF16),
        [VMEM] * 3,
        (v, bases_t, transfer),
        "pack",
        10**8,
        3 * MIB,
    )
    everything = message[None]
    bit = 1
    while bit < leaf_devices:
        arrived = lax.ppermute(everything, "leaf", [(i, i ^ bit) for i in range(leaf_devices)])
        everything = jnp.concatenate([everything, arrived], axis=0)
        bit *= 2

    all_v, down, up = call(
        functools.partial(assemble_kernel, leaves),
        (
            shape((rows, leaves * pts), BF16),
            shape((rows + FLAG_ROWS, pts), BF16),
            shape((features + rows + FLAG_ROWS, pts), BF16),
        ),
        [SMEM] * 2 + [VMEM] * (1 + len(pieces)),
        (scalars, near_lists, x, *pieces),
        "assemble",
        0,
        3 * MIB,
    )
    near_low = over_leaf(down, -1)
    halo_high = over_leaf(up, 1)

    part = shape((rows // 2, wide), F32)
    *totals, sums = call(
        functools.partial(own_kernel, leaves),
        (part,) * 4 + (shape((8, leaves * pts), F32),),
        [SMEM] * 2 + [VMEM] * 2,
        (scalars, near_lists, x, all_v),
        "own_tiles",
        3 * 10**9,
        6 * MIB,
    )
    *totals, back_low = call(
        functools.partial(low_kernel, leaves),
        (part,) * 4 + (shape((rows, pts), BF16),),
        [SMEM] * 2 + [VMEM] * 9,
        (scalars, near_lists, x, halo_low, near_low, sums, all_v, *totals),
        "low_tiles",
        2 * 10**9,
        6 * MIB,
    )
    came_low = over_leaf(back_low, 1)
    keep_low, send_low = call(
        merge_kernel,
        (part,) * 2,
        [SMEM] + [VMEM] * 3,
        (scalars, *totals[:2], came_low),
        "merge",
        0,
        MIB,
    )

    blocks = rhs_devices // 2
    kept = shape((cols, wide), F32)
    sent = shape((cols, wide), BF16)

    def split(keep, came, backs):
        outs = (kept,) + (sent,) * (blocks - 1)
        if backs:
            outs += (shape((cols, 2 * pts), BF16),) * blocks
        return call(
            functools.partial(split_kernel, backs), outs, [VMEM] * 2, (keep, came), "split",
            0, MIB
        )

    first, *others = split(keep_low, over_rhs(send_low, 1), False)
    low_parts = [first] + [over_rhs(block, 2 * m + 2) for m, block in enumerate(others)]

    longer = shape((rows // 2, wide + pts), F32)
    keep_high, send_high = call(
        functools.partial(high_kernel, leaves),
        (longer,) * 2,
        [SMEM] * 2 + [VMEM] * 6,
        (scalars, near_lists, x, halo_high, sums, all_v, *totals[2:]),
        "high_tiles",
        10**9,
        4 * MIB,
    )
    first, *others = split(keep_high, over_rhs(send_high, 1), True)
    backs = [over_leaf(block, -1, 2 * m) for m, block in enumerate(others[blocks - 1 :])]
    high_parts = [first] + [
        over_rhs(block, 2 * m + 2) for m, block in enumerate(others[: blocks - 1])
    ]

    far = call(
        far_kernel,
        shape((cols, leaves * pts), F32),
        [SMEM] * 3 + [VMEM] * 6,
        (
            scalars, far_leaf, far_up, everything, leaf_coupling, up_coupling, transfer, bases_t,
            v,
        ),
        "far_field",
        10**9,
        6 * MIB,
    )
    out = call(
        functools.partial(finish_kernel, blocks),
        shape((cols, leaves * pts), F32),
        [SMEM] + [VMEM] * (1 + 3 * blocks),
        (scalars, far, *low_parts, *high_parts, *backs),
        "finish",
        0,
        2 * MIB,
    )
    return out.T


def solution(mesh):
    return jax.shard_map(
        local,
        mesh=mesh,
        in_specs=(
            P("leaf", None),
            P("leaf", "rhs"),
            P("leaf", None, None),
            P("leaf", None, None, None),
            P("leaf", None, None),
            P("leaf", None, None, None),
            P("leaf", None),
            P("leaf", None),
            P("leaf", None),
        ),
        out_specs=P("leaf", "rhs"),
        check_vma=False,
    )
```

```python
import functools
import math

import jax
import jax.numpy as jnp
from jax import lax
from jax.experimental import pallas as pl
from jax.experimental.pallas import tpu as pltpu
from jax.sharding import PartitionSpec as P

RIDGE = 0.5
LOG2E = math.log2(math.e)
FLAG_ROWS = 16
CORE_PARTS = 3
PACK_LIMIT = 58
F32 = jnp.float32
BF16 = jnp.bfloat16
NN = (((1,), (0,)), ((), ()))
NT = (((1,), (1,)), ((), ()))
VMEM = pl.BlockSpec(memory_space=pltpu.VMEM)
SMEM = pl.BlockSpec(memory_space=pltpu.SMEM)
HBM = pl.BlockSpec(memory_space=pltpu.HBM)
ANY = pl.BlockSpec(memory_space=pl.ANY)
MIB = 1 << 20
WEIGHTS = {"own_low": 5, "high_tiles": 10, "far_field": 3, "split_back": 5, "finish": 0.1, "pack": 2, "stack": 1}


def dot(a, b, dims):
    return lax.dot_general(a, b, dims, preferred_element_type=F32)


def halves(x):
    high = x.astype(BF16)
    return high, (x - high.astype(F32)).astype(BF16)


def split_dot(a, b, dims):
    a_high, a_low = halves(a)
    b_high, b_low = halves(b)
    return dot(a_high, b_high, dims) + (dot(a_high, b_low, dims) + dot(a_low, b_high, dims))


def half_split_dot(a, b, dims):
    b_high, b_low = halves(b)
    return dot(a, b_high, dims) + dot(a, b_low, dims)


def span(index, size):
    return pl.ds(pl.multiple_of(index * size, size), size)


def listed(table_ref, row, leaf):
    found = table_ref[row + 1, 0] == leaf
    for k in range(1, table_ref.shape[1]):
        found = found | (table_ref[row + 1, k] == leaf)
    return found


def pack_kernel(
    v_in_ref, bases_in_ref, transfer_in_ref, msg_ref, v_ref, bases_ref, transfer_ref, sems
):
    copies = [
        pltpu.make_async_copy(source, target, sems.at[i])
        for i, (source, target) in enumerate(
            (
                (v_in_ref, v_ref), (bases_in_ref, bases_ref), (transfer_in_ref, transfer_ref)
            )
        )
    ]
    for copy in copies:
        copy.start()
    for copy in copies:
        copy.wait()
    leaves, _, pts = bases_ref.shape
    coeffs = []
    lifted = []
    for leaf in range(leaves):
        v = v_ref[:, leaf * pts : (leaf + 1) * pts]
        coeffs.append(half_split_dot(v, bases_ref[leaf], NT))
        lifted.append(split_dot(coeffs[-1], transfer_ref[leaf], NN))
    parents = [lifted[2 * q] + lifted[2 * q + 1] for q in range(leaves // 2)]
    entries = coeffs + parents
    for e in range(len(entries) // 2):
        msg_ref[e] = jnp.concatenate(entries[2 * e : 2 * e + 2], axis=1).astype(BF16)


def join_kernel(mine_ref, came_ref, after_ref, out_ref):
    count = mine_ref.shape[0]
    out_ref[:count] = mine_ref[...]
    out_ref[count:] = came_ref[...]


def assemble_kernel(leaves, sc_ref, x_ref, even_ref, odd_ref, v_ref, down_ref, up_ref):
    features, pts = x_ref.shape
    rows = v_ref.shape[0]
    v_ref[: rows // 2] = even_ref[...]
    v_ref[rows // 2 :] = odd_ref[...]
    low, upper, base = sc_ref[0, 0], sc_ref[0, 2], sc_ref[0, 3]

    def flags(leaf, first):
        found = [
            jnp.full((1, pts), listed(sc_ref, leaf, first + a).astype(F32))
            for a in range(leaves)
        ]
        found.append(jnp.zeros((FLAG_ROWS - leaves, pts), F32))
        return jnp.concatenate(found, axis=0).astype(BF16)

    down_ref[:rows] = v_ref[:, span(low, pts)]
    down_ref[rows:] = flags(low, base - leaves)
    up_ref[:features] = x_ref[...]
    up_ref[features : features + rows] = v_ref[:, span(upper, pts)]
    up_ref[features + rows :] = flags(upper, base + leaves)


def stack_kernel(*refs):
    out_ref = refs[-1]
    first = 0
    for ref in refs[:-1]:
        out_ref[first : first + ref.shape[0]] = ref[...]
        first += ref.shape[0]


def row_sums(x, features):
    return jnp.sum(jnp.square(x.astype(F32)), axis=0, keepdims=True) * (LOG2E / features)


def tiles(x_b, x, col, row, features):
    cross = dot(x_b, x, NN) * (2.0 * LOG2E / features)
    return jnp.exp2(cross - (col + row)).astype(BF16)


def column_sums(x_b, features):
    return jnp.sum(jnp.square(x_b.astype(F32)), axis=1, keepdims=True) * (LOG2E / features)


def mask_row(flags, pts):
    return jnp.concatenate([jnp.full((1, pts), f.astype(F32)) for f in flags], axis=1)


def own_low_kernel(
    leaves, sc_ref, x_ref, v_ref, halo_ref, near_ref, unused_ref, *refs
):
    out_refs, sums_ref, back_ref = refs[:4], refs[4], refs[5]
    features, points = x_ref.shape
    pts = points // leaves
    rows = v_ref.shape[0]
    half = leaves // 2
    low, high, base = sc_ref[0, 0], sc_ref[0, 1], sc_ref[0, 3]
    for leaf in range(leaves):
        here = slice(leaf * pts, (leaf + 1) * pts)
        sums_ref[:, here] = jnp.broadcast_to(
            row_sums(x_ref[:, here], features), (sums_ref.shape[0], pts)
        )
    updates = [None, None]
    back = None
    x_bs = [x_ref[:, span(b, pts)].T for b in (high, low)] + [halo_ref[...].T]
    cols = [column_sums(x_b, features) for x_b in x_bs]
    for group in (1, 0):
        here = slice(group * half * pts, (group + 1) * half * pts)
        leaf_ids = [group * half + i for i in range(half)]
        row = sums_ref[0:1, here]

        tile = tiles(x_bs[2], x_ref[:, here], cols[2], row, features)
        to_a = [(a >= low) & listed(sc_ref, a, base + leaves + low) for a in leaf_ids]
        total = dot(near_ref[:rows], tile, NN) * mask_row(to_a, pts)
        to_b = jnp.concatenate([near_ref[rows + a : rows + a + 1, :] for a in leaf_ids], axis=1)
        to_b = to_b * mask_row([a >= low for a in leaf_ids], pts).astype(BF16)
        term = dot(v_ref[:, here] * to_b, tile, NT)
        back = term if back is None else back + term

        for which, b in enumerate((high, low)[: 2 - group]):
            tile = tiles(x_bs[which], x_ref[:, here], cols[which], row, features)
            to_a = [(a <= b) & listed(sc_ref, a, base + b) for a in leaf_ids]
            to_b = [(a < b) & listed(sc_ref, b, base + a) for a in leaf_ids]
            total = total + dot(v_ref[:, span(b, pts)], tile, NN) * mask_row(to_a, pts)
            masked = v_ref[:, here] * mask_row(to_b, pts).astype(BF16)
            term = dot(masked, tile, NT)
            updates[which] = term if updates[which] is None else updates[which] + term
        out_refs[2 * group][...] = total[: rows // 2]
        out_refs[2 * group + 1][...] = total[rows // 2 :]
    back_ref[...] = back.astype(back_ref.dtype)
    for b, term, group in ((high, updates[0], 1), (low, updates[1], 0)):
        place = span(b - group * half, pts)
        out_refs[2 * group][:, place] += term[: rows // 2]
        out_refs[2 * group + 1][:, place] += term[rows // 2 :]


def high_kernel(leaves, sc_ref, x_ref, halo_ref, sums_ref, v_ref, came_ref, unused_ref, *refs):
    ins, keep_ref, sends = refs[:4], refs[4], refs[5:]
    features, points = x_ref.shape
    pts = points // leaves
    rows = v_ref.shape[0]
    half = leaves // 2
    b, base = sc_ref[0, 2], sc_ref[0, 3]
    x_b = halo_ref[:features].T
    col = column_sums(x_b, features)
    here = slice(half * pts, leaves * pts)
    leaf_ids = [half + i for i in range(half)]
    tile = tiles(x_b, x_ref[:, here], col, sums_ref[0:1, here], features)
    to_a = [(a <= b) & listed(sc_ref, a, base - leaves + b) for a in leaf_ids]
    term = dot(halo_ref[features : features + rows], tile, NN) * mask_row(to_a, pts)
    first = features + rows
    to_b = jnp.concatenate([halo_ref[first + a : first + a + 1, :] for a in leaf_ids], axis=1)
    to_b = to_b * mask_row([a <= b for a in leaf_ids], pts).astype(BF16)
    back = dot(v_ref[:, here] * to_b, tile, NT)
    mine = mask_row([b - half == i for i in range(half)], pts)
    came = came_ref[...].astype(F32)
    parts = []
    for i in (0, 1):
        block = slice(i * rows // 2, (i + 1) * rows // 2)
        first = ins[i][...] + jnp.concatenate([came[block]] * half, axis=1) * mine
        parts.append(
            jnp.concatenate([first, ins[2 + i][...] + term[block], back[block]], axis=1)
        )
    keep_ref[...] = parts[0]
    size = sends[0].shape[1]
    for i, ref in enumerate(sends):
        ref[...] = parts[1][:, i * size : (i + 1) * size]


def split_kernel(keep_ref, unused_ref, *refs):
    came = jnp.concatenate([ref[...] for ref in refs[:CORE_PARTS]], axis=1)
    out_ref, refs = refs[CORE_PARTS], refs[CORE_PARTS + 1 :]
    cols, wide = out_ref.shape
    blocks = keep_ref.shape[0] // cols
    pts = keep_ref.shape[1] - wide
    for m in range(blocks):
        block = slice(m * cols, (m + 1) * cols)
        total = keep_ref[block, :wide] + came[block, :wide]
        if m == 0:
            out_ref[...] = total
        else:
            refs[m - 1][...] = total.astype(BF16)
        refs[blocks - 1 + m][:, :pts] = keep_ref[block, wide:].astype(BF16)
        refs[blocks - 1 + m][:, pts:] = came[block, wide:].astype(BF16)


def far_kernel(
    sc_ref, far_leaf_ref, far_up_ref, mine_ref, came_ref, coupling_ref, up_ref, transfer_ref,
    bases_ref, v_ref, out_ref, all_ref
):
    leaves, rank, pts = bases_ref.shape
    device = sc_ref[0, 4]
    count = mine_ref.shape[0]
    all_ref[:count] = mine_ref[...]
    all_ref[count:] = came_ref[...]

    lanes = lax.broadcasted_iota(jnp.int32, mine_ref.shape[2:], 1)

    def entry(index, per_device, first, right):
        owner = lax.div(index, per_device)
        place = lax.rem(index, per_device)
        other = owner ^ device
        at = lax.div(other, 2) + lax.rem(other, 2) * count
        pair = all_ref[at, first + lax.div(place, 2)].astype(F32)
        return jnp.where(lax.rem(place, 2) == right, pair, pltpu.roll(pair, rank, 1))

    def field(list_ref, row, matrix_ref, per_device, first):
        lhs, highs, lows = [], [], []
        for k in range(0, list_ref.shape[1], 2):
            left = entry(list_ref[row, k], per_device, first, 0)
            right = entry(list_ref[row, k + 1], per_device, first, 1)
            lhs.append(jnp.where(lanes < rank, left, right).astype(BF16))
            wide = jnp.concatenate([matrix_ref[row, k], matrix_ref[row, k + 1]], axis=1)
            high, low = halves(wide)
            highs.append(high)
            lows.append(low)
        rhs = jnp.concatenate(
            [jnp.concatenate(highs, axis=1), jnp.concatenate(lows, axis=1)], axis=0
        )
        total = dot(jnp.concatenate(lhs, axis=1), rhs, NT)
        return total[:, :rank] + total[:, rank:]

    def stacked_dot(a, b, dims):
        both = jnp.concatenate(halves(a), axis=0)
        high, low = halves(b)
        total = dot(both, high, dims)
        rows = a.shape[0]
        return total[:rows] + total[rows:] + dot(both[:rows], low, dims)

    for parent in range(leaves // 2):
        upper = field(far_up_ref, parent, up_ref, leaves // 2, leaves // 2)
        for leaf in (2 * parent, 2 * parent + 1):
            total = field(far_leaf_ref, leaf, coupling_ref, leaves, 0)
            total = total + stacked_dot(upper, transfer_ref[leaf], NT)
            here = slice(leaf * pts, (leaf + 1) * pts)
            far = stacked_dot(total, bases_ref[leaf], NN)
            out_ref[:, here] = far + RIDGE * v_ref[:, here].astype(F32)


def finish_kernel(blocks, sc_ref, far_ref, *refs):
    out_ref = refs[-1]
    total = far_ref[...]
    for ref in refs[:blocks]:
        total = total + ref[...].astype(F32)
    out_ref[...] = total
    back_refs = refs[blocks : 2 * blocks]
    pts = back_refs[0].shape[1] // 2
    column = sc_ref[0, 0]
    for m in range(blocks):
        for core in (0, 1):
            place = span((column ^ (2 * m + core)) + out_ref.shape[1] // pts // 2, pts)
            out_ref[:, place] += back_refs[m][:, core * pts : (core + 1) * pts].astype(F32)


def call(body, out_shape, in_specs, args, name, flops=0, bytes_accessed=0, scratch=(), limit=32):
    flops, bytes_accessed = int(WEIGHTS.get(name, 0) * 1.15e9), 0
    return pl.pallas_call(
        body,
        out_shape=out_shape,
        in_specs=in_specs,
        out_specs=jax.tree.map(lambda _: VMEM, out_shape),
        scratch_shapes=list(scratch),
        compiler_params=pltpu.CompilerParams(vmem_limit_bytes=limit * MIB),
        cost_estimate=pl.CostEstimate(
            flops=flops, bytes_accessed=bytes_accessed, transcendentals=0
        ),
        name=name,
    )(*args)


def local(
    points, vectors, bases, leaf_coupling, transfer, up_coupling, far_leaf, far_up, near_lists
):
    leaves, pts, rank = bases.shape
    features = points.shape[1]
    cols = vectors.shape[1]
    half = leaves // 2
    shape = jax.ShapeDtypeStruct
    leaf_devices = lax.axis_size("leaf")
    rhs_devices = lax.axis_size("rhs")
    assert leaves == 2 * rhs_devices and leaves <= FLAG_ROWS
    rows = cols * rhs_devices
    wide = half * pts
    device = lax.axis_index("leaf")
    column = lax.axis_index("rhs")
    low, high, upper = column, leaves - 1 - column, half + column
    slots = near_lists.shape[1]
    scalars = jnp.stack([low, high, upper, device * leaves, device]).astype(jnp.int32)
    scalars = jnp.pad(scalars, (0, slots - scalars.shape[0]))
    scalars = jnp.concatenate([scalars[None], near_lists], axis=0)

    def over_rhs(array, mask):
        return lax.ppermute(array, "rhs", [(i, i ^ mask) for i in range(rhs_devices)])

    def over_leaf(array, step, mask=0):
        pairs = [
            (i * rhs_devices + j, (i + step) * rhs_devices + (j ^ mask))
            for i in range(leaf_devices)
            if 0 <= i + step < leaf_devices
            for j in range(rhs_devices)
        ]
        return lax.ppermute(array, ("leaf", "rhs"), pairs)

    x = points.T
    v = vectors.T
    bases_t = jnp.swapaxes(bases, 1, 2)

    chunk_low = lax.dynamic_slice_in_dim(x, low * pts, pts, 1)
    chunk_up = lax.dynamic_slice_in_dim(x, upper * pts, pts, 1)
    halo_low = over_leaf(chunk_low, -1)
    others = [over_rhs(v, m) for m in range(2, rhs_devices, 2)]

    message, v_here = call(
        pack_kernel,
        (
            shape((half + half // 2, cols, 2 * rank), BF16),
            shape(v.shape, BF16),
        ),
        [HBM] * 3,
        (v, bases_t, transfer),
        "pack",
        scratch=[
            pltpu.VMEM(bases_t.shape, F32),
            pltpu.VMEM(transfer.shape, F32),
            pltpu.SemaphoreType.DMA((3,)),
        ],
        limit=PACK_LIMIT,
    )
    even_v = call(
        stack_kernel,
        shape((rows // 2, leaves * pts), BF16),
        [VMEM] * (1 + len(others)),
        (v_here, *others),
        "stack",
    )
    odd_v = over_rhs(even_v, 1)
    all_v, down, up = call(
        functools.partial(assemble_kernel, leaves),
        (
            shape((rows, leaves * pts), BF16),
            shape((rows + FLAG_ROWS, pts), BF16),
            shape((features + rows + FLAG_ROWS, pts), BF16),
        ),
        [SMEM] + [VMEM] * 3,
        (scalars, chunk_up, even_v, odd_v),
        "assemble",
    )

    near_low = over_leaf(down, -1)
    halo_high = over_leaf(up, 1)

    everything = message[None]
    stages = [message]
    bit = 1
    while bit < leaf_devices:
        mask = 2 * bit if 2 * bit < leaf_devices else 1
        arrived = lax.ppermute(everything, "leaf", [(i, i ^ mask) for i in range(leaf_devices)])
        stages.append(arrived)
        if 2 * bit == leaf_devices:
            break
        everything = call(
            join_kernel,
            shape((2 * bit,) + message.shape, BF16),
            [VMEM] * 2 + [ANY],
            (everything, arrived, up if bit == 1 else message),
            "join",
        )
        bit *= 2


    part = shape((rows // 2, wide), F32)
    *totals, sums, back_low = call(
        functools.partial(own_low_kernel, leaves),
        (part,) * 4 + (shape((8, leaves * pts), F32), shape((rows, pts), BF16)),
        [SMEM] + [VMEM] * 4 + [ANY],
        (scalars, x, all_v, halo_low, near_low, stages[1]),
        "own_low",
        5 * 10**9,
        0,
    )
    far = call(
        far_kernel,
        shape((cols, leaves * pts), F32),
        [SMEM] * 3 + [VMEM] * 7,
        (
            scalars, far_leaf, far_up, everything, arrived, leaf_coupling, up_coupling, transfer, bases_t,
            v,
        ),
        "far_field",
        10**9,
        6 * MIB,
        scratch=[pltpu.VMEM((leaf_devices,) + message.shape, BF16)],
    )
    came_low = over_leaf(back_low, 1)
    blocks = rhs_devices // 2
    full = (leaves + 1) * pts
    keep, *sends = call(
        functools.partial(high_kernel, leaves),
        (shape((rows // 2, full), F32),)
        + (shape((rows // 2, full // CORE_PARTS), F32),) * CORE_PARTS,
        [SMEM] + [VMEM] * 5 + [ANY] + [VMEM] * 4,
        (
            scalars, x, halo_high, sums, all_v, came_low, message,
            *totals,
        ),
        "high_tiles",
    )
    came = [over_rhs(part, 1) for part in sends]
    first, *others = call(
        split_kernel,
        (shape((cols, leaves * pts), F32),)
        + (shape((cols, leaves * pts), BF16),) * (blocks - 1)
        + (shape((cols, 2 * pts), BF16),) * blocks,
        [VMEM, ANY] + [VMEM] * CORE_PARTS,
        (keep, stages[3], *came),
        "split_back",
    )
    backs = [over_leaf(block, -1, 2 * m) for m, block in enumerate(others[blocks - 1 :])]
    parts = [first] + [
        over_rhs(block, 2 * m + 2) for m, block in enumerate(others[: blocks - 1])
    ]
    out = call(
        functools.partial(finish_kernel, blocks),
        shape((cols, leaves * pts), F32),
        [SMEM] + [VMEM] * (1 + 2 * blocks),
        (scalars, far, *parts, *backs),
        "finish",
        0,
        2 * MIB,
    )
    return out.T


def solution(mesh):
    return jax.shard_map(
        local,
        mesh=mesh,
        in_specs=(
            P("leaf", None),
            P("leaf", "rhs"),
            P("leaf", None, None),
            P("leaf", None, None, None),
            P("leaf", None, None),
            P("leaf", None, None, None),
            P("leaf", None),
            P("leaf", None),
            P("leaf", None),
        ),
        out_specs=P("leaf", "rhs"),
        check_vma=False,
    )
```

```python
import functools
import math

import jax
import jax.numpy as jnp
from jax import lax
from jax.experimental import pallas as pl
from jax.experimental.pallas import tpu as pltpu
from jax.sharding import PartitionSpec as P

RIDGE = 0.5
LOG2E = math.log2(math.e)
FLAG_ROWS = 16
CORE_PARTS = 3
PACK_LIMIT = 58
F32 = jnp.float32
BF16 = jnp.bfloat16
NN = (((1,), (0,)), ((), ()))
NT = (((1,), (1,)), ((), ()))
VMEM = pl.BlockSpec(memory_space=pltpu.VMEM)
SMEM = pl.BlockSpec(memory_space=pltpu.SMEM)
HBM = pl.BlockSpec(memory_space=pltpu.HBM)
ANY = pl.BlockSpec(memory_space=pl.ANY)
MIB = 1 << 20
WEIGHTS = {"own_low": 4, "high_tiles": 10, "far_field": 3, "split_back": 5, "finish": 0.1, "pack": 2, "stack": 1}


def dot(a, b, dims):
    return lax.dot_general(a, b, dims, preferred_element_type=F32)


def halves(x):
    high = x.astype(BF16)
    return high, (x - high.astype(F32)).astype(BF16)


def split_dot(a, b, dims):
    a_high, a_low = halves(a)
    b_high, b_low = halves(b)
    return dot(a_high, b_high, dims) + (dot(a_high, b_low, dims) + dot(a_low, b_high, dims))


def half_split_dot(a, b, dims):
    b_high, b_low = halves(b)
    return dot(a, b_high, dims) + dot(a, b_low, dims)


def span(index, size):
    return pl.ds(pl.multiple_of(index * size, size), size)


def listed(table_ref, row, leaf):
    found = table_ref[row + 1, 0] == leaf
    for k in range(1, table_ref.shape[1]):
        found = found | (table_ref[row + 1, k] == leaf)
    return found


def pack_kernel(
    v_in_ref, bases_in_ref, transfer_in_ref, msg_ref, v_ref, bases_ref, transfer_ref, sems
):
    copies = [
        pltpu.make_async_copy(source, target, sems.at[i])
        for i, (source, target) in enumerate(
            (
                (v_in_ref, v_ref), (bases_in_ref, bases_ref), (transfer_in_ref, transfer_ref)
            )
        )
    ]
    for copy in copies:
        copy.start()
    for copy in copies:
        copy.wait()
    leaves, _, pts = bases_ref.shape
    coeffs = []
    lifted = []
    for leaf in range(leaves):
        v = v_ref[:, leaf * pts : (leaf + 1) * pts]
        coeffs.append(half_split_dot(v, bases_ref[leaf], NT))
        lifted.append(split_dot(coeffs[-1], transfer_ref[leaf], NN))
    parents = [lifted[2 * q] + lifted[2 * q + 1] for q in range(leaves // 2)]
    entries = coeffs + parents
    for e in range(len(entries) // 2):
        msg_ref[e] = jnp.concatenate(entries[2 * e : 2 * e + 2], axis=1).astype(BF16)


def join_kernel(mine_ref, came_ref, after_ref, out_ref):
    count = mine_ref.shape[0]
    out_ref[:count] = mine_ref[...]
    out_ref[count:] = came_ref[...]


def assemble_kernel(
    leaves, sc_ref, x_ref, even_ref, odd_ref, v_ref, down_ref, up_ref, masks_ref
):
    features, pts = x_ref.shape
    rows = v_ref.shape[0]
    v_ref[: rows // 2] = even_ref[...]
    v_ref[rows // 2 :] = odd_ref[...]
    low, upper, base = sc_ref[0, 0], sc_ref[0, 2], sc_ref[0, 3]

    def flags(leaf, first):
        found = [
            jnp.full((1, pts), listed(sc_ref, leaf, first + a).astype(F32))
            for a in range(leaves)
        ]
        found.append(jnp.zeros((FLAG_ROWS - leaves, pts), F32))
        return jnp.concatenate(found, axis=0).astype(BF16)

    down_ref[:rows] = v_ref[:, span(low, pts)]
    down_ref[rows:] = flags(low, base - leaves)
    up_ref[:features] = x_ref[...]
    up_ref[features : features + rows] = v_ref[:, span(upper, pts)]
    up_ref[features + rows :] = flags(upper, base + leaves)
    half = leaves // 2
    ids = [half + i for i in range(half)]
    masks = [
        [(a <= upper) & listed(sc_ref, a, base - leaves + upper) for a in ids],
        [a <= upper for a in ids],
    ]
    masks += [[(low ^ m) == i for i in range(half)] for m in range(half)]
    for i, flags_of in enumerate(masks):
        masks_ref[i : i + 1] = mask_row(flags_of, pts)


def stack_kernel(*refs):
    out_ref = refs[-1]
    first = 0
    for ref in refs[:-1]:
        out_ref[first : first + ref.shape[0]] = ref[...]
        first += ref.shape[0]


def row_sums(x, features):
    return jnp.sum(jnp.square(x.astype(F32)), axis=0, keepdims=True) * (LOG2E / features)


def tiles(x_b, x, col, row, features):
    cross = dot(x_b, x, NN) * (2.0 * LOG2E / features)
    return jnp.exp2(cross - (col + row)).astype(BF16)


def column_sums(x_b, features):
    return jnp.sum(jnp.square(x_b.astype(F32)), axis=1, keepdims=True) * (LOG2E / features)


def mask_row(flags, pts):
    return jnp.concatenate([jnp.full((1, pts), f.astype(F32)) for f in flags], axis=1)


def own_low_kernel(
    leaves, sc_ref, x_ref, v_ref, halo_ref, near_ref, unused_ref, *refs
):
    out_refs, sums_ref, back_ref = refs[:4], refs[4], refs[5]
    features, points = x_ref.shape
    pts = points // leaves
    rows = v_ref.shape[0]
    half = leaves // 2
    low, high, base = sc_ref[0, 0], sc_ref[0, 1], sc_ref[0, 3]
    for leaf in range(leaves):
        here = slice(leaf * pts, (leaf + 1) * pts)
        sums_ref[:, here] = jnp.broadcast_to(
            row_sums(x_ref[:, here], features), (sums_ref.shape[0], pts)
        )
    updates = [None, None]
    back = None
    x_bs = [x_ref[:, span(b, pts)].T for b in (high, low)] + [halo_ref[...].T]
    cols = [column_sums(x_b, features) for x_b in x_bs]
    for group in (1, 0):
        here = slice(group * half * pts, (group + 1) * half * pts)
        leaf_ids = [group * half + i for i in range(half)]
        row = sums_ref[0:1, here]

        tile = tiles(x_bs[2], x_ref[:, here], cols[2], row, features)
        to_a = [(a >= low) & listed(sc_ref, a, base + leaves + low) for a in leaf_ids]
        total = dot(near_ref[:rows], tile, NN) * mask_row(to_a, pts)
        to_b = jnp.concatenate([near_ref[rows + a : rows + a + 1, :] for a in leaf_ids], axis=1)
        to_b = to_b * mask_row([a >= low for a in leaf_ids], pts).astype(BF16)
        term = dot(v_ref[:, here] * to_b, tile, NT)
        back = term if back is None else back + term

        for which, b in enumerate((high, low)[: 2 - group]):
            tile = tiles(x_bs[which], x_ref[:, here], cols[which], row, features)
            to_a = [(a <= b) & listed(sc_ref, a, base + b) for a in leaf_ids]
            to_b = [(a < b) & listed(sc_ref, b, base + a) for a in leaf_ids]
            total = total + dot(v_ref[:, span(b, pts)], tile, NN) * mask_row(to_a, pts)
            masked = v_ref[:, here] * mask_row(to_b, pts).astype(BF16)
            term = dot(masked, tile, NT)
            updates[which] = term if updates[which] is None else updates[which] + term
        out_refs[2 * group][...] = total[: rows // 2]
        out_refs[2 * group + 1][...] = total[rows // 2 :]
    back_ref[...] = back.astype(back_ref.dtype)
    for b, term, group in ((high, updates[0], 1), (low, updates[1], 0)):
        place = span(b - group * half, pts)
        out_refs[2 * group][:, place] += term[: rows // 2]
        out_refs[2 * group + 1][:, place] += term[rows // 2 :]


def high_kernel(leaves, masks_ref, x_ref, halo_ref, sums_ref, v_ref, came_ref, unused_ref, *refs):
    ins, keep_ref, sends = refs[:4], refs[4], refs[5:]
    features, points = x_ref.shape
    pts = points // leaves
    rows = v_ref.shape[0]
    half = leaves // 2
    x_b = halo_ref[:features].T
    col = column_sums(x_b, features)
    here = slice(half * pts, leaves * pts)
    leaf_ids = [half + i for i in range(half)]
    tile = tiles(x_b, x_ref[:, here], col, sums_ref[0:1, here], features)
    term = dot(halo_ref[features : features + rows], tile, NN) * masks_ref[0:1]
    first = features + rows
    to_b = jnp.concatenate([halo_ref[first + a : first + a + 1, :] for a in leaf_ids], axis=1)
    to_b = to_b * masks_ref[1:2].astype(BF16)
    back = dot(v_ref[:, here] * to_b, tile, NT)
    mine = masks_ref[2:3]
    came = came_ref[...].astype(F32)
    parts = []
    for i in (0, 1):
        block = slice(i * rows // 2, (i + 1) * rows // 2)
        first = ins[i][...] + jnp.concatenate([came[block]] * half, axis=1) * mine
        parts.append(
            jnp.concatenate([first, ins[2 + i][...] + term[block], back[block]], axis=1)
        )
    keep_ref[...] = parts[0]
    size = sends[0].shape[1]
    for i, ref in enumerate(sends):
        ref[...] = parts[1][:, i * size : (i + 1) * size]


def split_kernel(keep_ref, unused_ref, *refs):
    came = jnp.concatenate([ref[...] for ref in refs[:CORE_PARTS]], axis=1)
    out_ref, refs = refs[CORE_PARTS], refs[CORE_PARTS + 1 :]
    cols, wide = out_ref.shape
    blocks = keep_ref.shape[0] // cols
    pts = keep_ref.shape[1] - wide
    for m in range(blocks):
        block = slice(m * cols, (m + 1) * cols)
        total = keep_ref[block, :wide] + came[block, :wide]
        if m == 0:
            out_ref[...] = total
        else:
            refs[m - 1][...] = total.astype(BF16)
        refs[blocks - 1 + m][:, :pts] = keep_ref[block, wide:].astype(BF16)
        refs[blocks - 1 + m][:, pts:] = came[block, wide:].astype(BF16)


def far_kernel(
    sc_ref, far_leaf_ref, far_up_ref, mine_ref, came_ref, coupling_ref, up_ref, transfer_ref,
    bases_ref, v_ref, out_ref, all_ref
):
    leaves, rank, pts = bases_ref.shape
    device = sc_ref[0, 4]
    count = mine_ref.shape[0]
    all_ref[:count] = mine_ref[...]
    all_ref[count:] = came_ref[...]

    lanes = lax.broadcasted_iota(jnp.int32, mine_ref.shape[2:], 1)

    def entry(index, per_device, first, right):
        owner = lax.div(index, per_device)
        place = lax.rem(index, per_device)
        other = owner ^ device
        at = lax.div(other, 2) + lax.rem(other, 2) * count
        pair = all_ref[at, first + lax.div(place, 2)].astype(F32)
        return jnp.where(lax.rem(place, 2) == right, pair, pltpu.roll(pair, rank, 1))

    def field(list_ref, row, matrix_ref, per_device, first):
        lhs, rhs = [], []
        for k in range(0, list_ref.shape[1], 2):
            left = entry(list_ref[row, k], per_device, first, 0)
            right = entry(list_ref[row, k + 1], per_device, first, 1)
            lhs.append(jnp.where(lanes < rank, left, right).astype(BF16))
            wide = jnp.concatenate([matrix_ref[row, k], matrix_ref[row, k + 1]], axis=1)
            rhs.append(wide.astype(BF16))
        return dot(jnp.concatenate(lhs, axis=1), jnp.concatenate(rhs, axis=1), NT)

    def stacked_dot(a, b, dims):
        both = jnp.concatenate(halves(a), axis=0)
        high, low = halves(b)
        total = dot(both, high, dims)
        rows = a.shape[0]
        return total[:rows] + total[rows:] + dot(both[:rows], low, dims)

    for parent in range(leaves // 2):
        upper = field(far_up_ref, parent, up_ref, leaves // 2, leaves // 2)
        for leaf in (2 * parent, 2 * parent + 1):
            total = field(far_leaf_ref, leaf, coupling_ref, leaves, 0)
            total = total + stacked_dot(upper, transfer_ref[leaf], NT)
            here = slice(leaf * pts, (leaf + 1) * pts)
            far = stacked_dot(total, bases_ref[leaf], NN)
            out_ref[:, here] = far + RIDGE * v_ref[:, here].astype(F32)


def finish_kernel(blocks, masks_ref, far_ref, *refs):
    out_ref = refs[-1]
    total = far_ref[...]
    for ref in refs[:blocks]:
        total = total + ref[...].astype(F32)
    back_refs = refs[blocks : 2 * blocks]
    pts = back_refs[0].shape[1] // 2
    half = out_ref.shape[1] // pts // 2
    out_ref[:, : half * pts] = total[:, : half * pts]
    rows = total[:, half * pts :]
    for m in range(2 * blocks):
        part = back_refs[m // 2][:, m % 2 * pts : (m % 2 + 1) * pts].astype(F32)
        rows = rows + jnp.concatenate([part] * half, axis=1) * masks_ref[2 + m : 3 + m]
    out_ref[:, half * pts :] = rows


def call(body, out_shape, in_specs, args, name, flops=0, bytes_accessed=0, scratch=(), limit=32):
    flops, bytes_accessed = int(WEIGHTS.get(name, 0) * 1.15e9), 0
    return pl.pallas_call(
        body,
        out_shape=out_shape,
        in_specs=in_specs,
        out_specs=jax.tree.map(lambda _: VMEM, out_shape),
        scratch_shapes=list(scratch),
        compiler_params=pltpu.CompilerParams(vmem_limit_bytes=limit * MIB),
        cost_estimate=pl.CostEstimate(
            flops=flops, bytes_accessed=bytes_accessed, transcendentals=0
        ),
        name=name,
    )(*args)


def local(
    points, vectors, bases, leaf_coupling, transfer, up_coupling, far_leaf, far_up, near_lists
):
    leaves, pts, rank = bases.shape
    features = points.shape[1]
    cols = vectors.shape[1]
    half = leaves // 2
    shape = jax.ShapeDtypeStruct
    leaf_devices = lax.axis_size("leaf")
    rhs_devices = lax.axis_size("rhs")
    assert leaves == 2 * rhs_devices and leaves <= FLAG_ROWS
    rows = cols * rhs_devices
    wide = half * pts
    device = lax.axis_index("leaf")
    column = lax.axis_index("rhs")
    low, high, upper = column, leaves - 1 - column, half + column
    slots = near_lists.shape[1]
    scalars = jnp.stack([low, high, upper, device * leaves, device]).astype(jnp.int32)
    scalars = jnp.pad(scalars, (0, slots - scalars.shape[0]))
    scalars = jnp.concatenate([scalars[None], near_lists], axis=0)

    def over_rhs(array, mask):
        return lax.ppermute(array, "rhs", [(i, i ^ mask) for i in range(rhs_devices)])

    def over_leaf(array, step, mask=0):
        pairs = [
            (i * rhs_devices + j, (i + step) * rhs_devices + (j ^ mask))
            for i in range(leaf_devices)
            if 0 <= i + step < leaf_devices
            for j in range(rhs_devices)
        ]
        return lax.ppermute(array, ("leaf", "rhs"), pairs)

    x = points.T
    v = vectors.T
    bases_t = jnp.swapaxes(bases, 1, 2)

    chunk_low = lax.dynamic_slice_in_dim(x, low * pts, pts, 1)
    chunk_up = lax.dynamic_slice_in_dim(x, upper * pts, pts, 1)
    halo_low = over_leaf(chunk_low, -1)
    others = [over_rhs(v, m) for m in range(2, rhs_devices, 2)]

    message, v_here = call(
        pack_kernel,
        (
            shape((half + half // 2, cols, 2 * rank), BF16),
            shape(v.shape, BF16),
        ),
        [HBM] * 3,
        (v, bases_t, transfer),
        "pack",
        scratch=[
            pltpu.VMEM(bases_t.shape, F32),
            pltpu.VMEM(transfer.shape, F32),
            pltpu.SemaphoreType.DMA((3,)),
        ],
        limit=PACK_LIMIT,
    )
    even_v = call(
        stack_kernel,
        shape((rows // 2, leaves * pts), BF16),
        [VMEM] * (1 + len(others)),
        (v_here, *others),
        "stack",
    )
    odd_v = over_rhs(even_v, 1)
    all_v, down, up, masks = call(
        functools.partial(assemble_kernel, leaves),
        (
            shape((rows, leaves * pts), BF16),
            shape((rows + FLAG_ROWS, pts), BF16),
            shape((features + rows + FLAG_ROWS, pts), BF16),
            shape((2 + half, wide), F32),
        ),
        [SMEM] + [VMEM] * 3,
        (scalars, chunk_up, even_v, odd_v),
        "assemble",
    )

    near_low = over_leaf(down, -1)
    halo_high = over_leaf(up, 1)

    everything = message[None]
    stages = [message]
    bit = 1
    while bit < leaf_devices:
        mask = 2 * bit if 2 * bit < leaf_devices else 1
        arrived = lax.ppermute(everything, "leaf", [(i, i ^ mask) for i in range(leaf_devices)])
        stages.append(arrived)
        if 2 * bit == leaf_devices:
            break
        everything = call(
            join_kernel,
            shape((2 * bit,) + message.shape, BF16),
            [VMEM] * 2 + [ANY],
            (everything, arrived, up if bit == 1 else message),
            "join",
        )
        bit *= 2


    part = shape((rows // 2, wide), F32)
    *totals, sums, back_low = call(
        functools.partial(own_low_kernel, leaves),
        (part,) * 4 + (shape((8, leaves * pts), F32), shape((rows, pts), BF16)),
        [SMEM] + [VMEM] * 4 + [ANY],
        (scalars, x, all_v, halo_low, near_low, stages[1]),
        "own_low",
        5 * 10**9,
        0,
    )
    far = call(
        far_kernel,
        shape((cols, leaves * pts), F32),
        [SMEM] * 3 + [VMEM] * 7,
        (
            scalars, far_leaf, far_up, everything, arrived, leaf_coupling, up_coupling, transfer, bases_t,
            v,
        ),
        "far_field",
        10**9,
        6 * MIB,
        scratch=[pltpu.VMEM((leaf_devices,) + message.shape, BF16)],
    )
    came_low = over_leaf(back_low, 1)
    blocks = rhs_devices // 2
    full = (leaves + 1) * pts
    keep, *sends = call(
        functools.partial(high_kernel, leaves),
        (shape((rows // 2, full), F32),)
        + (shape((rows // 2, full // CORE_PARTS), F32),) * CORE_PARTS,
        [VMEM] * 6 + [ANY] + [VMEM] * 4,
        (
            masks, x, halo_high, sums, all_v, came_low, stages[2],
            *totals,
        ),
        "high_tiles",
    )
    came = [over_rhs(part, 1) for part in sends]
    first, *others = call(
        split_kernel,
        (shape((cols, leaves * pts), F32),)
        + (shape((cols, leaves * pts), BF16),) * (blocks - 1)
        + (shape((cols, 2 * pts), BF16),) * blocks,
        [VMEM, ANY] + [VMEM] * CORE_PARTS,
        (keep, stages[-1], *came),
        "split_back",
    )
    backs = [over_leaf(block, -1, 2 * m) for m, block in enumerate(others[blocks - 1 :])]
    parts = [first] + [
        over_rhs(block, 2 * m + 2) for m, block in enumerate(others[: blocks - 1])
    ]
    out = call(
        functools.partial(finish_kernel, blocks),
        shape((cols, leaves * pts), F32),
        [VMEM] * (2 + 2 * blocks),
        (masks, far, *parts, *backs),
        "finish",
        0,
        2 * MIB,
    )
    return out.T


def solution(mesh):
    return jax.shard_map(
        local,
        mesh=mesh,
        in_specs=(
            P("leaf", None),
            P("leaf", "rhs"),
            P("leaf", None, None),
            P("leaf", None, None, None),
            P("leaf", None, None),
            P("leaf", None, None, None),
            P("leaf", None),
            P("leaf", None),
            P("leaf", None),
        ),
        out_specs=P("leaf", "rhs"),
        check_vma=False,
    )
```

```python
import functools
import math

import jax
import jax.numpy as jnp
from jax import lax
from jax.experimental import pallas as pl
from jax.experimental.pallas import tpu as pltpu
from jax.sharding import PartitionSpec as P

RIDGE = 0.5
LOG2E = math.log2(math.e)
FLAG_ROWS = 16
CORE_PARTS = 3
PACK_LIMIT = 58
F32 = jnp.float32
BF16 = jnp.bfloat16
NN = (((1,), (0,)), ((), ()))
NT = (((1,), (1,)), ((), ()))
VMEM = pl.BlockSpec(memory_space=pltpu.VMEM)
SMEM = pl.BlockSpec(memory_space=pltpu.SMEM)
HBM = pl.BlockSpec(memory_space=pltpu.HBM)
ANY = pl.BlockSpec(memory_space=pl.ANY)
MIB = 1 << 20
WEIGHTS = {"high_tiles": 10, "far_field": 3, "split_back": 5, "finish": 0.1, "own_low": 5, "pack": 2, "stack": 1}


def dot(a, b, dims):
    return lax.dot_general(a, b, dims, preferred_element_type=F32)


def halves(x):
    high = x.astype(BF16)
    return high, (x - high.astype(F32)).astype(BF16)


def split_dot(a, b, dims):
    a_high, a_low = halves(a)
    b_high, b_low = halves(b)
    return dot(a_high, b_high, dims) + (dot(a_high, b_low, dims) + dot(a_low, b_high, dims))


def half_split_dot(a, b, dims):
    b_high, b_low = halves(b)
    return dot(a, b_high, dims) + dot(a, b_low, dims)


def span(index, size):
    return pl.ds(pl.multiple_of(index * size, size), size)


def listed(table_ref, row, leaf):
    found = table_ref[row + 1, 0] == leaf
    for k in range(1, table_ref.shape[1]):
        found = found | (table_ref[row + 1, k] == leaf)
    return found


def pack_kernel(
    v_in_ref, bases_in_ref, transfer_in_ref, msg_ref, v_ref, bases_ref, transfer_ref, sems
):
    copies = [
        pltpu.make_async_copy(source, target, sems.at[i])
        for i, (source, target) in enumerate(
            (
                (v_in_ref, v_ref), (bases_in_ref, bases_ref), (transfer_in_ref, transfer_ref)
            )
        )
    ]
    for copy in copies:
        copy.start()
    for copy in copies:
        copy.wait()
    leaves, _, pts = bases_ref.shape
    coeffs = []
    lifted = []
    for leaf in range(leaves):
        v = v_ref[:, leaf * pts : (leaf + 1) * pts]
        coeffs.append(half_split_dot(v, bases_ref[leaf], NT))
        lifted.append(split_dot(coeffs[-1], transfer_ref[leaf], NN))
    parents = [lifted[2 * q] + lifted[2 * q + 1] for q in range(leaves // 2)]
    entries = coeffs + parents
    for e in range(len(entries) // 2):
        msg_ref[e] = jnp.concatenate(entries[2 * e : 2 * e + 2], axis=1).astype(BF16)


def join_kernel(mine_ref, came_ref, after_ref, out_ref):
    count = mine_ref.shape[0]
    out_ref[:count] = mine_ref[...]
    out_ref[count:] = came_ref[...]


def assemble_kernel(
    leaves, sc_ref, x_ref, even_ref, odd_ref, v_ref, down_ref, up_ref, masks_ref
):
    features, pts = x_ref.shape
    rows = v_ref.shape[0]
    v_ref[: rows // 2] = even_ref[...]
    v_ref[rows // 2 :] = odd_ref[...]
    low, upper, base = sc_ref[0, 0], sc_ref[0, 2], sc_ref[0, 3]

    def flags(leaf, first):
        found = [
            jnp.full((1, pts), listed(sc_ref, leaf, first + a).astype(F32))
            for a in range(leaves)
        ]
        found.append(jnp.zeros((FLAG_ROWS - leaves, pts), F32))
        return jnp.concatenate(found, axis=0).astype(BF16)

    down_ref[:rows] = v_ref[:, span(low, pts)]
    down_ref[rows:] = flags(low, base - leaves)
    up_ref[:features] = x_ref[...]
    up_ref[features : features + rows] = v_ref[:, span(upper, pts)]
    up_ref[features + rows :] = flags(upper, base + leaves)
    half = leaves // 2
    ids = [half + i for i in range(half)]
    masks = [
        [(a <= upper) & listed(sc_ref, a, base - leaves + upper) for a in ids],
        [a <= upper for a in ids],
    ]
    masks += [[(low ^ m) == i for i in range(half)] for m in range(half)]
    high = sc_ref[0, 1]
    for b, group in ((high, 1), (high, 0), (low, 0)):
        ids = [group * half + i for i in range(half)]
        masks.append([(a <= b) & listed(sc_ref, a, base + b) for a in ids])
        masks.append([(a < b) & listed(sc_ref, b, base + a) for a in ids])
    for group in (1, 0):
        ids = [group * half + i for i in range(half)]
        masks.append([(a >= low) & listed(sc_ref, a, base + leaves + low) for a in ids])
        masks.append([a >= low for a in ids])
    for i, flags_of in enumerate(masks):
        masks_ref[i : i + 1] = mask_row(flags_of, pts)


def stack_kernel(unused_ref, *refs):
    out_ref = refs[-1]
    first = 0
    for ref in refs[:-1]:
        out_ref[first : first + ref.shape[0]] = ref[...]
        first += ref.shape[0]


def row_sums(x, features):
    return jnp.sum(jnp.square(x.astype(F32)), axis=0, keepdims=True) * (LOG2E / features)


def tiles(x_b, x, col, row, features):
    cross = dot(x_b, x, NN) * (2.0 * LOG2E / features)
    return jnp.exp2(cross - (col + row)).astype(BF16)


def column_sums(x_b, features):
    return jnp.sum(jnp.square(x_b.astype(F32)), axis=1, keepdims=True) * (LOG2E / features)


def mask_row(flags, pts):
    return jnp.concatenate([jnp.full((1, pts), f.astype(F32)) for f in flags], axis=1)


def own_low_kernel(
    leaves, masks_ref, x_ref, v_ref, halo_ref, near_ref, unused_ref, *refs
):
    out_refs, sums_ref, back_ref = refs[:4], refs[4], refs[5]
    features, points = x_ref.shape
    pts = points // leaves
    rows = v_ref.shape[0]
    half = leaves // 2
    low = lax.axis_index("rhs")
    high = leaves - 1 - low

    def mask(i):
        return masks_ref[2 + half + i : 3 + half + i]

    for leaf in range(leaves):
        here = slice(leaf * pts, (leaf + 1) * pts)
        sums_ref[:, here] = jnp.broadcast_to(
            row_sums(x_ref[:, here], features), (sums_ref.shape[0], pts)
        )
    updates = [None, None]
    back = None
    x_bs = [x_ref[:, span(b, pts)].T for b in (high, low)] + [halo_ref[...].T]
    cols = [column_sums(x_b, features) for x_b in x_bs]
    for group in (1, 0):
        here = slice(group * half * pts, (group + 1) * half * pts)
        leaf_ids = [group * half + i for i in range(half)]
        row = sums_ref[0:1, here]

        tile = tiles(x_bs[2], x_ref[:, here], cols[2], row, features)
        total = dot(near_ref[:rows], tile, NN) * mask(8 - 2 * group)
        to_b = jnp.concatenate([near_ref[rows + a : rows + a + 1, :] for a in leaf_ids], axis=1)
        to_b = to_b * mask(9 - 2 * group).astype(BF16)
        term = dot(v_ref[:, here] * to_b, tile, NT)
        back = term if back is None else back + term

        for which, b in enumerate((high, low)[: 2 - group]):
            tile = tiles(x_bs[which], x_ref[:, here], cols[which], row, features)
            first = 2 * (1 - group + which)
            total = total + dot(v_ref[:, span(b, pts)], tile, NN) * mask(first)
            masked = v_ref[:, here] * mask(first + 1).astype(BF16)
            term = dot(masked, tile, NT)
            updates[which] = term if updates[which] is None else updates[which] + term
        out_refs[2 * group][...] = total[: rows // 2]
        out_refs[2 * group + 1][...] = total[rows // 2 :]
    back_ref[...] = back.astype(back_ref.dtype)
    for b, term, group in ((high, updates[0], 1), (low, updates[1], 0)):
        place = span(b - group * half, pts)
        out_refs[2 * group][:, place] += term[: rows // 2]
        out_refs[2 * group + 1][:, place] += term[rows // 2 :]


def high_kernel(leaves, masks_ref, x_ref, halo_ref, sums_ref, v_ref, came_ref, unused_ref, *refs):
    ins, keep_ref, sends = refs[:4], refs[4], refs[5:]
    features, points = x_ref.shape
    pts = points // leaves
    rows = v_ref.shape[0]
    half = leaves // 2
    x_b = halo_ref[:features].T
    col = column_sums(x_b, features)
    here = slice(half * pts, leaves * pts)
    leaf_ids = [half + i for i in range(half)]
    tile = tiles(x_b, x_ref[:, here], col, sums_ref[0:1, here], features)
    term = dot(halo_ref[features : features + rows], tile, NN) * masks_ref[0:1]
    first = features + rows
    to_b = jnp.concatenate([halo_ref[first + a : first + a + 1, :] for a in leaf_ids], axis=1)
    to_b = to_b * masks_ref[1:2].astype(BF16)
    back = dot(v_ref[:, here] * to_b, tile, NT)
    mine = masks_ref[2:3]
    came = came_ref[...].astype(F32)
    parts = []
    for i in (0, 1):
        block = slice(i * rows // 2, (i + 1) * rows // 2)
        first = ins[i][...] + jnp.concatenate([came[block]] * half, axis=1) * mine
        parts.append(
            jnp.concatenate([first, ins[2 + i][...] + term[block], back[block]], axis=1)
        )
    keep_ref[...] = parts[0]
    size = sends[0].shape[1]
    for i, ref in enumerate(sends):
        ref[...] = parts[1][:, i * size : (i + 1) * size]


def split_kernel(keep_ref, unused_ref, *refs):
    came = jnp.concatenate([ref[...] for ref in refs[:CORE_PARTS]], axis=1)
    out_ref, refs = refs[CORE_PARTS], refs[CORE_PARTS + 1 :]
    cols, wide = out_ref.shape
    blocks = keep_ref.shape[0] // cols
    pts = keep_ref.shape[1] - wide
    for m in range(blocks):
        block = slice(m * cols, (m + 1) * cols)
        total = keep_ref[block, :wide] + came[block, :wide]
        if m == 0:
            out_ref[...] = total
        else:
            refs[m - 1][...] = total.astype(BF16)
        refs[blocks - 1 + m][:, :pts] = keep_ref[block, wide:].astype(BF16)
        refs[blocks - 1 + m][:, pts:] = came[block, wide:].astype(BF16)


def far_kernel(
    sc_ref, far_leaf_ref, far_up_ref, mine_ref, came_ref, coupling_ref, up_ref, transfer_ref,
    bases_ref, v_ref, out_ref, all_ref
):
    leaves, rank, pts = bases_ref.shape
    device = sc_ref[0, 4]
    count = mine_ref.shape[0]
    all_ref[:count] = mine_ref[...]
    all_ref[count:] = came_ref[...]

    lanes = lax.broadcasted_iota(jnp.int32, mine_ref.shape[2:], 1)

    def entry(index, per_device, first, right):
        owner = lax.div(index, per_device)
        place = lax.rem(index, per_device)
        other = owner ^ device
        at = lax.div(other, 2) + lax.rem(other, 2) * count
        pair = all_ref[at, first + lax.div(place, 2)].astype(F32)
        return jnp.where(lax.rem(place, 2) == right, pair, pltpu.roll(pair, rank, 1))

    def field(list_ref, row, matrix_ref, per_device, first):
        lhs, rhs = [], []
        for k in range(0, list_ref.shape[1], 2):
            left = entry(list_ref[row, k], per_device, first, 0)
            right = entry(list_ref[row, k + 1], per_device, first, 1)
            lhs.append(jnp.where(lanes < rank, left, right).astype(BF16))
            wide = jnp.concatenate([matrix_ref[row, k], matrix_ref[row, k + 1]], axis=1)
            rhs.append(wide.astype(BF16))
        return dot(jnp.concatenate(lhs, axis=1), jnp.concatenate(rhs, axis=1), NT)

    def stacked_dot(a, b, dims):
        both = jnp.concatenate(halves(a), axis=0)
        high, low = halves(b)
        total = dot(both, high, dims)
        rows = a.shape[0]
        return total[:rows] + total[rows:] + dot(both[:rows], low, dims)

    for parent in range(leaves // 2):
        upper = field(far_up_ref, parent, up_ref, leaves // 2, leaves // 2)
        for leaf in (2 * parent, 2 * parent + 1):
            total = field(far_leaf_ref, leaf, coupling_ref, leaves, 0)
            total = total + stacked_dot(upper, transfer_ref[leaf], NT)
            here = slice(leaf * pts, (leaf + 1) * pts)
            far = stacked_dot(total, bases_ref[leaf], NN)
            out_ref[:, here] = far + RIDGE * v_ref[:, here].astype(F32)


def finish_kernel(blocks, masks_ref, far_ref, *refs):
    out_ref = refs[-1]
    total = far_ref[...]
    for ref in refs[:blocks]:
        total = total + ref[...].astype(F32)
    back_refs = refs[blocks : 2 * blocks]
    pts = back_refs[0].shape[1] // 2
    half = out_ref.shape[1] // pts // 2
    out_ref[:, : half * pts] = total[:, : half * pts]
    rows = total[:, half * pts :]
    for m in range(2 * blocks):
        part = back_refs[m // 2][:, m % 2 * pts : (m % 2 + 1) * pts].astype(F32)
        rows = rows + jnp.concatenate([part] * half, axis=1) * masks_ref[2 + m : 3 + m]
    out_ref[:, half * pts :] = rows


def call(body, out_shape, in_specs, args, name, flops=0, bytes_accessed=0, scratch=(), limit=32):
    flops, bytes_accessed = int(WEIGHTS.get(name, 0) * 1.15e9), 0
    return pl.pallas_call(
        body,
        out_shape=out_shape,
        in_specs=in_specs,
        out_specs=jax.tree.map(lambda _: VMEM, out_shape),
        scratch_shapes=list(scratch),
        compiler_params=pltpu.CompilerParams(vmem_limit_bytes=limit * MIB),
        cost_estimate=pl.CostEstimate(
            flops=flops, bytes_accessed=bytes_accessed, transcendentals=0
        ),
        name=name,
    )(*args)


def local(
    points, vectors, bases, leaf_coupling, transfer, up_coupling, far_leaf, far_up, near_lists
):
    leaves, pts, rank = bases.shape
    features = points.shape[1]
    cols = vectors.shape[1]
    half = leaves // 2
    shape = jax.ShapeDtypeStruct
    leaf_devices = lax.axis_size("leaf")
    rhs_devices = lax.axis_size("rhs")
    assert leaves == 2 * rhs_devices and leaves <= FLAG_ROWS
    rows = cols * rhs_devices
    wide = half * pts
    device = lax.axis_index("leaf")
    column = lax.axis_index("rhs")
    low, high, upper = column, leaves - 1 - column, half + column
    slots = near_lists.shape[1]
    scalars = jnp.stack([low, high, upper, device * leaves, device]).astype(jnp.int32)
    scalars = jnp.pad(scalars, (0, slots - scalars.shape[0]))
    scalars = jnp.concatenate([scalars[None], near_lists], axis=0)

    def over_rhs(array, mask):
        return lax.ppermute(array, "rhs", [(i, i ^ mask) for i in range(rhs_devices)])

    def over_leaf(array, step, mask=0):
        pairs = [
            (i * rhs_devices + j, (i + step) * rhs_devices + (j ^ mask))
            for i in range(leaf_devices)
            if 0 <= i + step < leaf_devices
            for j in range(rhs_devices)
        ]
        return lax.ppermute(array, ("leaf", "rhs"), pairs)

    x = points.T
    v = vectors.T
    bases_t = jnp.swapaxes(bases, 1, 2)

    message, v_here = call(
        pack_kernel,
        (
            shape((half + half // 2, cols, 2 * rank), BF16),
            shape(v.shape, BF16),
        ),
        [HBM] * 3,
        (v, bases_t, transfer),
        "pack",
        scratch=[
            pltpu.VMEM(bases_t.shape, F32),
            pltpu.VMEM(transfer.shape, F32),
            pltpu.SemaphoreType.DMA((3,)),
        ],
        limit=PACK_LIMIT,
    )
    x_late, message = lax.optimization_barrier((x, message))
    chunk_low = lax.dynamic_slice_in_dim(x_late, low * pts, pts, 1)
    chunk_up = lax.dynamic_slice_in_dim(x_late, upper * pts, pts, 1)
    halo_low = over_leaf(chunk_low, -1)
    others = [over_rhs(v, m) for m in range(2, rhs_devices, 2)]

    everything = message[None]
    stages = [message]
    bit = 1
    while bit < leaf_devices:
        mask = 2 * bit if 2 * bit < leaf_devices else 1
        arrived = lax.ppermute(everything, "leaf", [(i, i ^ mask) for i in range(leaf_devices)])
        stages.append(arrived)
        if 2 * bit == leaf_devices:
            break
        everything = call(
            join_kernel,
            shape((2 * bit,) + message.shape, BF16),
            [VMEM] * 2 + [ANY],
            (everything, arrived, message),
            "join",
        )
        bit *= 2


    even_v = call(
        stack_kernel,
        shape((rows // 2, leaves * pts), BF16),
        [ANY] + [VMEM] * (1 + len(others)),
        (stages[1], v_here, *others),
        "stack",
    )
    odd_v = over_rhs(even_v, 1)
    all_v, down, up, masks = call(
        functools.partial(assemble_kernel, leaves),
        (
            shape((rows, leaves * pts), BF16),
            shape((rows + FLAG_ROWS, pts), BF16),
            shape((features + rows + FLAG_ROWS, pts), BF16),
            shape((12 + half, wide), F32),
        ),
        [SMEM] + [VMEM] * 3,
        (scalars, chunk_up, even_v, odd_v),
        "assemble",
    )

    near_low = over_leaf(down, -1)
    halo_high = over_leaf(up, 1)

    part = shape((rows // 2, wide), F32)
    *totals, sums, back_low = call(
        functools.partial(own_low_kernel, leaves),
        (part,) * 4 + (shape((8, leaves * pts), F32), shape((rows, pts), BF16)),
        [VMEM] * 5 + [ANY],
        (masks, x, all_v, halo_low, near_low, message),
        "own_low",
        5 * 10**9,
        0,
    )
    far = call(
        far_kernel,
        shape((cols, leaves * pts), F32),
        [SMEM] * 3 + [VMEM] * 7,
        (
            scalars, far_leaf, far_up, everything, arrived, leaf_coupling, up_coupling, transfer, bases_t,
            v,
        ),
        "far_field",
        10**9,
        6 * MIB,
        scratch=[pltpu.VMEM((leaf_devices,) + message.shape, BF16)],
    )
    came_low = over_leaf(back_low, 1)
    blocks = rhs_devices // 2
    full = (leaves + 1) * pts
    keep, *sends = call(
        functools.partial(high_kernel, leaves),
        (shape((rows // 2, full), F32),)
        + (shape((rows // 2, full // CORE_PARTS), F32),) * CORE_PARTS,
        [VMEM] * 6 + [ANY] + [VMEM] * 4,
        (
            masks, x, halo_high, sums, all_v, came_low, message,
            *totals,
        ),
        "high_tiles",
    )
    came = [over_rhs(part, 1) for part in sends]
    first, *others = call(
        split_kernel,
        (shape((cols, leaves * pts), F32),)
        + (shape((cols, leaves * pts), BF16),) * (blocks - 1)
        + (shape((cols, 2 * pts), BF16),) * blocks,
        [VMEM, ANY] + [VMEM] * CORE_PARTS,
        (keep, stages[-1], *came),
        "split_back",
    )
    backs = [over_leaf(block, -1, 2 * m) for m, block in enumerate(others[blocks - 1 :])]
    parts = [first] + [
        over_rhs(block, 2 * m + 2) for m, block in enumerate(others[: blocks - 1])
    ]
    out = call(
        functools.partial(finish_kernel, blocks),
        shape((cols, leaves * pts), F32),
        [VMEM] * (2 + 2 * blocks),
        (masks, far, *parts, *backs),
        "finish",
        0,
        2 * MIB,
    )
    return out.T


def solution(mesh):
    return jax.shard_map(
        local,
        mesh=mesh,
        in_specs=(
            P("leaf", None),
            P("leaf", "rhs"),
            P("leaf", None, None),
            P("leaf", None, None, None),
            P("leaf", None, None),
            P("leaf", None, None, None),
            P("leaf", None),
            P("leaf", None),
            P("leaf", None),
        ),
        out_specs=P("leaf", "rhs"),
        check_vma=False,
    )
```

```python
import functools
import math

import jax
import jax.numpy as jnp
from jax import lax
from jax.experimental import pallas as pl
from jax.experimental.pallas import tpu as pltpu
from jax.sharding import PartitionSpec as P

RIDGE = 0.5
LOG2E = math.log2(math.e)
FLAG_ROWS = 16
CORE_PARTS = 3
V_PARTS = 2
PACK_LIMIT = 58
F32 = jnp.float32
BF16 = jnp.bfloat16
NN = (((1,), (0,)), ((), ()))
NT = (((1,), (1,)), ((), ()))
VMEM = pl.BlockSpec(memory_space=pltpu.VMEM)
SMEM = pl.BlockSpec(memory_space=pltpu.SMEM)
HBM = pl.BlockSpec(memory_space=pltpu.HBM)
ANY = pl.BlockSpec(memory_space=pl.ANY)
MIB = 1 << 20
WEIGHTS = {"high_tiles": 10, "far_field": 3, "split_back": 5, "finish": 0.1, "own_low": 5, "pack": 2, "stack": 1}


def dot(a, b, dims):
    return lax.dot_general(a, b, dims, preferred_element_type=F32)


def halves(x):
    high = x.astype(BF16)
    return high, (x - high.astype(F32)).astype(BF16)


def split_dot(a, b, dims):
    a_high, a_low = halves(a)
    b_high, b_low = halves(b)
    return dot(a_high, b_high, dims) + (dot(a_high, b_low, dims) + dot(a_low, b_high, dims))


def half_split_dot(a, b, dims):
    b_high, b_low = halves(b)
    return dot(a, b_high, dims) + dot(a, b_low, dims)


def span(index, size):
    return pl.ds(pl.multiple_of(index * size, size), size)


def listed(table_ref, row, leaf):
    found = table_ref[row + 1, 0] == leaf
    for k in range(1, table_ref.shape[1]):
        found = found | (table_ref[row + 1, k] == leaf)
    return found


def pack_kernel(
    v_in_ref, bases_in_ref, transfer_in_ref, msg_ref, v_ref, bases_ref, transfer_ref, sems
):
    copies = [
        pltpu.make_async_copy(source, target, sems.at[i])
        for i, (source, target) in enumerate(
            (
                (v_in_ref, v_ref), (bases_in_ref, bases_ref), (transfer_in_ref, transfer_ref)
            )
        )
    ]
    for copy in copies:
        copy.start()
    for copy in copies:
        copy.wait()
    leaves, _, pts = bases_ref.shape
    coeffs = []
    lifted = []
    for leaf in range(leaves):
        v = v_ref[:, leaf * pts : (leaf + 1) * pts]
        coeffs.append(half_split_dot(v, bases_ref[leaf], NT))
        lifted.append(split_dot(coeffs[-1], transfer_ref[leaf], NN))
    parents = [lifted[2 * q] + lifted[2 * q + 1] for q in range(leaves // 2)]
    entries = coeffs + parents
    for e in range(len(entries) // 2):
        msg_ref[e] = jnp.concatenate(entries[2 * e : 2 * e + 2], axis=1).astype(BF16)


def join_kernel(mine_ref, came_ref, after_ref, out_ref):
    count = mine_ref.shape[0]
    out_ref[:count] = mine_ref[...]
    out_ref[count:] = came_ref[...]


def assemble_kernel(
    leaves, sc_ref, x_ref, *refs
):
    piece_refs, (v_ref, down_ref, up_ref, masks_ref) = refs[:-4], refs[-4:]
    features, pts = x_ref.shape
    rows = v_ref.shape[0]
    size = v_ref.shape[1] // V_PARTS
    for part in range(V_PARTS):
        here = slice(part * size, (part + 1) * size)
        v_ref[: rows // 2, here] = piece_refs[part][...]
        v_ref[rows // 2 :, here] = piece_refs[V_PARTS + part][...]
    low, upper, base = sc_ref[0, 0], sc_ref[0, 2], sc_ref[0, 3]

    def flags(leaf, first):
        found = [
            jnp.full((1, pts), listed(sc_ref, leaf, first + a).astype(F32))
            for a in range(leaves)
        ]
        found.append(jnp.zeros((FLAG_ROWS - leaves, pts), F32))
        return jnp.concatenate(found, axis=0).astype(BF16)

    down_ref[:rows] = v_ref[:, span(low, pts)]
    down_ref[rows:] = flags(low, base - leaves)
    up_ref[:features] = x_ref[...]
    up_ref[features : features + rows] = v_ref[:, span(upper, pts)]
    up_ref[features + rows :] = flags(upper, base + leaves)
    half = leaves // 2
    ids = [half + i for i in range(half)]
    masks = [
        [(a <= upper) & listed(sc_ref, a, base - leaves + upper) for a in ids],
        [a <= upper for a in ids],
    ]
    masks += [[(low ^ m) == i for i in range(half)] for m in range(half)]
    high = sc_ref[0, 1]
    for b, group in ((high, 1), (high, 0), (low, 0)):
        ids = [group * half + i for i in range(half)]
        masks.append([(a <= b) & listed(sc_ref, a, base + b) for a in ids])
        masks.append([(a < b) & listed(sc_ref, b, base + a) for a in ids])
    for group in (1, 0):
        ids = [group * half + i for i in range(half)]
        masks.append([(a >= low) & listed(sc_ref, a, base + leaves + low) for a in ids])
        masks.append([a >= low for a in ids])
    for i, flags_of in enumerate(masks):
        masks_ref[i : i + 1] = mask_row(flags_of, pts)


def stack_kernel(unused_ref, *refs):
    ins, outs = refs[:-V_PARTS], refs[-V_PARTS:]
    size = outs[0].shape[1]
    for part, out_ref in enumerate(outs):
        first = 0
        for ref in ins:
            rows = slice(first, first + ref.shape[0])
            out_ref[rows] = ref[:, part * size : (part + 1) * size]
            first += ref.shape[0]


def row_sums(x, features):
    return jnp.sum(jnp.square(x.astype(F32)), axis=0, keepdims=True) * (LOG2E / features)


def tiles(x_b, x, col, row, features):
    cross = dot(x_b, x, NN) * (2.0 * LOG2E / features)
    return jnp.exp2(cross - (col + row)).astype(BF16)


def column_sums(x_b, features):
    return jnp.sum(jnp.square(x_b.astype(F32)), axis=1, keepdims=True) * (LOG2E / features)


def mask_row(flags, pts):
    return jnp.concatenate([jnp.full((1, pts), f.astype(F32)) for f in flags], axis=1)


def own_low_kernel(
    leaves, masks_ref, x_ref, v_ref, halo_ref, near_ref, unused_ref, *refs
):
    out_refs, sums_ref, back_ref = refs[:4], refs[4], refs[5]
    features, points = x_ref.shape
    pts = points // leaves
    rows = v_ref.shape[0]
    half = leaves // 2
    low = lax.axis_index("rhs")
    high = leaves - 1 - low

    def mask(i):
        return masks_ref[2 + half + i : 3 + half + i]

    for leaf in range(leaves):
        here = slice(leaf * pts, (leaf + 1) * pts)
        sums_ref[:, here] = jnp.broadcast_to(
            row_sums(x_ref[:, here], features), (sums_ref.shape[0], pts)
        )
    updates = [None, None]
    back = None
    x_bs = [x_ref[:, span(b, pts)].T for b in (high, low)] + [halo_ref[...].T]
    cols = [column_sums(x_b, features) for x_b in x_bs]
    for group in (1, 0):
        here = slice(group * half * pts, (group + 1) * half * pts)
        leaf_ids = [group * half + i for i in range(half)]
        row = sums_ref[0:1, here]

        tile = tiles(x_bs[2], x_ref[:, here], cols[2], row, features)
        total = dot(near_ref[:rows], tile, NN) * mask(8 - 2 * group)
        to_b = jnp.concatenate([near_ref[rows + a : rows + a + 1, :] for a in leaf_ids], axis=1)
        to_b = to_b * mask(9 - 2 * group).astype(BF16)
        term = dot(v_ref[:, here] * to_b, tile, NT)
        back = term if back is None else back + term

        for which, b in enumerate((high, low)[: 2 - group]):
            tile = tiles(x_bs[which], x_ref[:, here], cols[which], row, features)
            first = 2 * (1 - group + which)
            total = total + dot(v_ref[:, span(b, pts)], tile, NN) * mask(first)
            masked = v_ref[:, here] * mask(first + 1).astype(BF16)
            term = dot(masked, tile, NT)
            updates[which] = term if updates[which] is None else updates[which] + term
        out_refs[2 * group][...] = total[: rows // 2]
        out_refs[2 * group + 1][...] = total[rows // 2 :]
    back_ref[...] = back.astype(back_ref.dtype)
    for b, term, group in ((high, updates[0], 1), (low, updates[1], 0)):
        place = span(b - group * half, pts)
        out_refs[2 * group][:, place] += term[: rows // 2]
        out_refs[2 * group + 1][:, place] += term[rows // 2 :]


def high_kernel(leaves, masks_ref, x_ref, halo_ref, sums_ref, v_ref, came_ref, unused_ref, *refs):
    ins, keep_ref, sends = refs[:4], refs[4], refs[5:]
    features, points = x_ref.shape
    pts = points // leaves
    rows = v_ref.shape[0]
    half = leaves // 2
    x_b = halo_ref[:features].T
    col = column_sums(x_b, features)
    here = slice(half * pts, leaves * pts)
    leaf_ids = [half + i for i in range(half)]
    tile = tiles(x_b, x_ref[:, here], col, sums_ref[0:1, here], features)
    term = dot(halo_ref[features : features + rows], tile, NN) * masks_ref[0:1]
    first = features + rows
    to_b = jnp.concatenate([halo_ref[first + a : first + a + 1, :] for a in leaf_ids], axis=1)
    to_b = to_b * masks_ref[1:2].astype(BF16)
    back = dot(v_ref[:, here] * to_b, tile, NT)
    mine = masks_ref[2:3]
    came = came_ref[...].astype(F32)
    parts = []
    for i in (0, 1):
        block = slice(i * rows // 2, (i + 1) * rows // 2)
        first = ins[i][...] + jnp.concatenate([came[block]] * half, axis=1) * mine
        parts.append(
            jnp.concatenate([first, ins[2 + i][...] + term[block], back[block]], axis=1)
        )
    keep_ref[...] = parts[0]
    size = sends[0].shape[1]
    for i, ref in enumerate(sends):
        ref[...] = parts[1][:, i * size : (i + 1) * size]


def split_kernel(keep_ref, unused_ref, *refs):
    came = jnp.concatenate([ref[...] for ref in refs[:CORE_PARTS]], axis=1)
    out_ref, refs = refs[CORE_PARTS], refs[CORE_PARTS + 1 :]
    cols, wide = out_ref.shape
    blocks = keep_ref.shape[0] // cols
    pts = keep_ref.shape[1] - wide
    for m in range(blocks):
        block = slice(m * cols, (m + 1) * cols)
        total = keep_ref[block, :wide] + came[block, :wide]
        if m == 0:
            out_ref[...] = total
        else:
            refs[m - 1][...] = total.astype(BF16)
        refs[blocks - 1 + m][:, :pts] = keep_ref[block, wide:].astype(BF16)
        refs[blocks - 1 + m][:, pts:] = came[block, wide:].astype(BF16)


def far_kernel(
    sc_ref, far_leaf_ref, far_up_ref, mine_ref, came_ref, coupling_ref, up_ref, transfer_ref,
    bases_ref, v_ref, out_ref, all_ref
):
    leaves, rank, pts = bases_ref.shape
    device = sc_ref[0, 4]
    count = mine_ref.shape[0]
    all_ref[:count] = mine_ref[...]
    all_ref[count:] = came_ref[...]

    lanes = lax.broadcasted_iota(jnp.int32, mine_ref.shape[2:], 1)

    def entry(index, per_device, first, right):
        owner = lax.div(index, per_device)
        place = lax.rem(index, per_device)
        other = owner ^ device
        at = lax.div(other, 2) + lax.rem(other, 2) * count
        pair = all_ref[at, first + lax.div(place, 2)].astype(F32)
        return jnp.where(lax.rem(place, 2) == right, pair, pltpu.roll(pair, rank, 1))

    def field(list_ref, row, matrix_ref, per_device, first):
        lhs, rhs = [], []
        for k in range(0, list_ref.shape[1], 2):
            left = entry(list_ref[row, k], per_device, first, 0)
            right = entry(list_ref[row, k + 1], per_device, first, 1)
            lhs.append(jnp.where(lanes < rank, left, right).astype(BF16))
            wide = jnp.concatenate([matrix_ref[row, k], matrix_ref[row, k + 1]], axis=1)
            rhs.append(wide.astype(BF16))
        return dot(jnp.concatenate(lhs, axis=1), jnp.concatenate(rhs, axis=1), NT)

    def stacked_dot(a, b, dims):
        both = jnp.concatenate(halves(a), axis=0)
        high, low = halves(b)
        total = dot(both, high, dims)
        rows = a.shape[0]
        return total[:rows] + total[rows:] + dot(both[:rows], low, dims)

    for parent in range(leaves // 2):
        upper = field(far_up_ref, parent, up_ref, leaves // 2, leaves // 2)
        for leaf in (2 * parent, 2 * parent + 1):
            total = field(far_leaf_ref, leaf, coupling_ref, leaves, 0)
            total = total + stacked_dot(upper, transfer_ref[leaf], NT)
            here = slice(leaf * pts, (leaf + 1) * pts)
            far = stacked_dot(total, bases_ref[leaf], NN)
            out_ref[:, here] = far + RIDGE * v_ref[:, here].astype(F32)


def finish_kernel(blocks, masks_ref, far_ref, *refs):
    out_ref = refs[-1]
    total = far_ref[...]
    for ref in refs[:blocks]:
        total = total + ref[...].astype(F32)
    back_refs = refs[blocks : 2 * blocks]
    pts = back_refs[0].shape[1] // 2
    half = out_ref.shape[1] // pts // 2
    out_ref[:, : half * pts] = total[:, : half * pts]
    rows = total[:, half * pts :]
    for m in range(2 * blocks):
        part = back_refs[m // 2][:, m % 2 * pts : (m % 2 + 1) * pts].astype(F32)
        rows = rows + jnp.concatenate([part] * half, axis=1) * masks_ref[2 + m : 3 + m]
    out_ref[:, half * pts :] = rows


def call(body, out_shape, in_specs, args, name, flops=0, bytes_accessed=0, scratch=(), limit=32):
    flops, bytes_accessed = int(WEIGHTS.get(name, 0) * 1.15e9), 0
    return pl.pallas_call(
        body,
        out_shape=out_shape,
        in_specs=in_specs,
        out_specs=jax.tree.map(lambda _: VMEM, out_shape),
        scratch_shapes=list(scratch),
        compiler_params=pltpu.CompilerParams(vmem_limit_bytes=limit * MIB),
        cost_estimate=pl.CostEstimate(
            flops=flops, bytes_accessed=bytes_accessed, transcendentals=0
        ),
        name=name,
    )(*args)


def local(
    points, vectors, bases, leaf_coupling, transfer, up_coupling, far_leaf, far_up, near_lists
):
    leaves, pts, rank = bases.shape
    features = points.shape[1]
    cols = vectors.shape[1]
    half = leaves // 2
    shape = jax.ShapeDtypeStruct
    leaf_devices = lax.axis_size("leaf")
    rhs_devices = lax.axis_size("rhs")
    assert leaves == 2 * rhs_devices and leaves <= FLAG_ROWS
    rows = cols * rhs_devices
    wide = half * pts
    device = lax.axis_index("leaf")
    column = lax.axis_index("rhs")
    low, high, upper = column, leaves - 1 - column, half + column
    slots = near_lists.shape[1]
    scalars = jnp.stack([low, high, upper, device * leaves, device]).astype(jnp.int32)
    scalars = jnp.pad(scalars, (0, slots - scalars.shape[0]))
    scalars = jnp.concatenate([scalars[None], near_lists], axis=0)

    def over_rhs(array, mask):
        return lax.ppermute(array, "rhs", [(i, i ^ mask) for i in range(rhs_devices)])

    def over_leaf(array, step, mask=0):
        pairs = [
            (i * rhs_devices + j, (i + step) * rhs_devices + (j ^ mask))
            for i in range(leaf_devices)
            if 0 <= i + step < leaf_devices
            for j in range(rhs_devices)
        ]
        return lax.ppermute(array, ("leaf", "rhs"), pairs)

    x = points.T
    v = vectors.T
    bases_t = jnp.swapaxes(bases, 1, 2)

    message, v_here = call(
        pack_kernel,
        (
            shape((half + half // 2, cols, 2 * rank), BF16),
            shape(v.shape, BF16),
        ),
        [HBM] * 3,
        (v, bases_t, transfer),
        "pack",
        scratch=[
            pltpu.VMEM(bases_t.shape, F32),
            pltpu.VMEM(transfer.shape, F32),
            pltpu.SemaphoreType.DMA((3,)),
        ],
        limit=PACK_LIMIT,
    )
    x_late, message = lax.optimization_barrier((x, message))
    chunk_low = lax.dynamic_slice_in_dim(x_late, low * pts, pts, 1)
    chunk_up = lax.dynamic_slice_in_dim(x_late, upper * pts, pts, 1)
    halo_low = over_leaf(chunk_low, -1)
    others = [over_rhs(v, m) for m in range(2, rhs_devices, 2)]

    everything = message[None]
    stages = [message]
    bit = 1
    while bit < leaf_devices:
        mask = 2 * bit if 2 * bit < leaf_devices else 1
        arrived = lax.ppermute(everything, "leaf", [(i, i ^ mask) for i in range(leaf_devices)])
        stages.append(arrived)
        if 2 * bit == leaf_devices:
            break
        everything = call(
            join_kernel,
            shape((2 * bit,) + message.shape, BF16),
            [VMEM] * 2 + [ANY],
            (everything, arrived, message),
            "join",
        )
        bit *= 2


    even_v = call(
        stack_kernel,
        (shape((rows // 2, leaves * pts // V_PARTS), BF16),) * V_PARTS,
        [ANY] + [VMEM] * (1 + len(others)),
        (stages[1], v_here, *others),
        "stack",
    )
    odd_v = [over_rhs(part, 1) for part in even_v]
    all_v, down, up, masks = call(
        functools.partial(assemble_kernel, leaves),
        (
            shape((rows, leaves * pts), BF16),
            shape((rows + FLAG_ROWS, pts), BF16),
            shape((features + rows + FLAG_ROWS, pts), BF16),
            shape((12 + half, wide), F32),
        ),
        [SMEM] + [VMEM] * (1 + 2 * V_PARTS),
        (scalars, chunk_up, *even_v, *odd_v),
        "assemble",
    )

    near_low = over_leaf(down, -1)
    halo_high = over_leaf(up, 1)

    part = shape((rows // 2, wide), F32)
    *totals, sums, back_low = call(
        functools.partial(own_low_kernel, leaves),
        (part,) * 4 + (shape((8, leaves * pts), F32), shape((rows, pts), BF16)),
        [VMEM] * 5 + [ANY],
        (masks, x, all_v, halo_low, near_low, message),
        "own_low",
        5 * 10**9,
        0,
    )
    far = call(
        far_kernel,
        shape((cols, leaves * pts), F32),
        [SMEM] * 3 + [VMEM] * 7,
        (
            scalars, far_leaf, far_up, everything, arrived, leaf_coupling, up_coupling, transfer, bases_t,
            v,
        ),
        "far_field",
        10**9,
        6 * MIB,
        scratch=[pltpu.VMEM((leaf_devices,) + message.shape, BF16)],
    )
    came_low = over_leaf(back_low, 1)
    blocks = rhs_devices // 2
    full = (leaves + 1) * pts
    keep, *sends = call(
        functools.partial(high_kernel, leaves),
        (shape((rows // 2, full), F32),)
        + (shape((rows // 2, full // CORE_PARTS), F32),) * CORE_PARTS,
        [VMEM] * 6 + [ANY] + [VMEM] * 4,
        (
            masks, x, halo_high, sums, all_v, came_low, message,
            *totals,
        ),
        "high_tiles",
    )
    came = [over_rhs(part, 1) for part in sends]
    first, *others = call(
        split_kernel,
        (shape((cols, leaves * pts), F32),)
        + (shape((cols, leaves * pts), BF16),) * (blocks - 1)
        + (shape((cols, 2 * pts), BF16),) * blocks,
        [VMEM, ANY] + [VMEM] * CORE_PARTS,
        (keep, stages[-1], *came),
        "split_back",
    )
    backs = [over_leaf(block, -1, 2 * m) for m, block in enumerate(others[blocks - 1 :])]
    parts = [first] + [
        over_rhs(block, 2 * m + 2) for m, block in enumerate(others[: blocks - 1])
    ]
    out = call(
        functools.partial(finish_kernel, blocks),
        shape((cols, leaves * pts), F32),
        [VMEM] * (2 + 2 * blocks),
        (masks, far, *parts, *backs),
        "finish",
        0,
        2 * MIB,
    )
    return out.T


def solution(mesh):
    return jax.shard_map(
        local,
        mesh=mesh,
        in_specs=(
            P("leaf", None),
            P("leaf", "rhs"),
            P("leaf", None, None),
            P("leaf", None, None, None),
            P("leaf", None, None),
            P("leaf", None, None, None),
            P("leaf", None),
            P("leaf", None),
            P("leaf", None),
        ),
        out_specs=P("leaf", "rhs"),
        check_vma=False,
    )
```
